256 devices in a mesh: grp: 2 (over core), seq: 32 (over z, y), tp: 4 (over x).
Axes of the slice: x: 4, y: 4, z: 8, core: 2. Of those that a mesh axis runs over, the one named last changes fastest.
Arguments:
- states: bfloat16 [24576, 4096], P('seq', 'tp'), may hold values from -24 to 24
- projections: bfloat16 [2, 4096, 2048], P('grp', None, 'tp'), may hold values from -0.09375 to 0.09375
- neighbours: bfloat16 [768, 64, 2048], P('seq', None, 'tp'), may hold values from -24 to 24
- owner: int32 [384, 2], P('seq'), may hold values from 0 to 31, as said below
- slot: int32 [384, 2], P('seq'), may hold values from 0 to 23, as said below
- cotangent: bfloat16 [24576, 2048], P('seq', 'tp'), may hold values from -48 to 48
Outputs:
- grad_states: bfloat16 [24576, 4096], P('seq', ('grp', 'tp'))
The draws below stay inside these ranges and needn't reach their ends.
Inputs may be any that keep to these rules, and one draw needn't show every extreme that they name: Each owner receives exactly 24 neighbours over all groups. Among the 24 neighbours of one decoder shard, one owner appears exactly 2 times and the other owners as nearly equally often as possible. The pair (owner, slot) names each of the 768 neighbours exactly once.
All inputs are finite; a program needn't handle non-finite values.
Results may differ from the reference program's by a relative error of at most 0.02.
The reference program's roundings to bfloat16 on the way count: a program that leaves them out, or rounds other values in their place, can miss the bound.
Values may be sent and summed in bfloat16 or wider, within the bound.
No kernel may reach another device: no remote copies, remote signals or barrier semaphores. Data moves between devices by JAX's collectives and lax.ppermute only.
A program may use at most 128 MiB of HBM per device.

```python
import jax
import jax.numpy as jnp
from jax import lax

DW = 4096
HD = 128
GROUP = 64
KNB = 2
HEADS = 16
NLEN = 64
HE = 2048
CH_DEV = 12
NB_DEV = 24
CAP = 2
TOKENS = 24576
GROUPS = 384
NEIGHS = 768
N_SEQ = 32


def routing_tables(key):
    row_key, col_key, offset_key, order_key, slot_key = jax.random.split(key, 5)
    row_perm = jax.random.permutation(row_key, N_SEQ)
    col_perm = jax.random.permutation(col_key, N_SEQ)
    remaining = NB_DEV - CAP
    offset_index = jnp.arange(N_SEQ)
    even_share = remaining // (N_SEQ - 1) + (offset_index - 1 < remaining % (N_SEQ - 1)).astype(jnp.int32)
    base_counts = jnp.where(offset_index == 0, CAP, even_share)
    base_counts = base_counts[jax.random.permutation(offset_key, N_SEQ)]
    offset = (col_perm[None, :] - row_perm[:, None]) % N_SEQ
    counts = base_counts[offset]
    bounds = jnp.cumsum(counts, axis=1)
    position = jnp.arange(NB_DEV)
    owners = jnp.sum((bounds[:, None, :] <= position[None, :, None]).astype(jnp.int32), axis=2)
    shuffles = jax.vmap(lambda row_seed: jax.random.permutation(row_seed, NB_DEV))(jax.random.split(order_key, N_SEQ))
    owners = jnp.take_along_axis(owners, shuffles, axis=1)
    flat_owners = owners.reshape(NEIGHS)
    priority = jax.random.permutation(slot_key, NEIGHS)
    ahead_mask = (flat_owners[None, :] == flat_owners[:, None]) & (priority[None, :] < priority[:, None])
    slots = jnp.sum(ahead_mask.astype(jnp.int32), axis=1)
    return (flat_owners.reshape(GROUPS, KNB).astype(jnp.int32), slots.reshape(GROUPS, KNB).astype(jnp.int32))


def draw_owner(key, part):
    return routing_tables(key)[0]


def draw_slot(key, part):
    return routing_tables(key)[1]


def spiked_rows(key, shape):
    value_key = jax.random.fold_in(key, 0)
    values = jax.random.normal(value_key, shape, jnp.float32)
    values = jnp.clip(values, -6.0, 6.0)
    return values


def draw_states(key, part):
    key = jax.random.fold_in(key, 11)
    return spiked_rows(key, (TOKENS, DW)).astype(jnp.bfloat16)


def draw_neighbours(key, part):
    key = jax.random.fold_in(key, 23)
    return spiked_rows(key, (NEIGHS, NLEN, HE)).astype(jnp.bfloat16)


def steps_of(key, shape, cuts, low, top_value):
    gain = 1.0
    for dim, parts in cuts:
        heights = jax.random.uniform(jax.random.fold_in(jax.random.fold_in(key, 6), dim), (parts,), jnp.float32, low / len(cuts), top_value / len(cuts))
        gain = gain * jnp.repeat(jnp.exp(heights), shape[dim] // parts).reshape((-1,) + (1,) * (len(shape) - 1 - dim))
    return gain


def bell_draw(stream_key, extent, deviation, limit, cuts=(), kind=jnp.bfloat16):
    factor_of = steps_of(stream_key, extent, cuts, -0.22, 0.18) if cuts else 1.0
    drawn = jax.random.normal(stream_key, extent, jnp.float32) * deviation * factor_of
    return jnp.minimum(jnp.maximum(drawn, -limit), limit).astype(kind)


def setup_inputs(seed: int = 0) -> dict:
    seeds = jax.random.split(jax.random.key(seed), 7)
    return {
        "states": draw_states(jax.random.fold_in(seeds[6], 71), 0),
        "projections": bell_draw(seeds[1], (2, DW, HE), DW ** -0.5, 0.09375, ((0, 2), (2, 4))),
        "neighbours": draw_neighbours(jax.random.fold_in(seeds[6], 71), 0),
        "owner": draw_owner(jax.random.fold_in(seeds[6], 71), 0),
        "slot": draw_slot(jax.random.fold_in(seeds[6], 71), 0),
        "cotangent": bell_draw(seeds[5], (TOKENS, HE), 8.0, 48.0, ((0, 32), (1, 4))),
    }


def split_heads(features):
    return features.reshape(features.shape[:-1] + (HEADS, HD))


def rounded(values):
    return lax.optimization_barrier(values.astype(jnp.bfloat16)).astype(jnp.float32)


def encode_forward(inputs, memory):
    score_scale = HD ** -0.5
    input_heads = split_heads(inputs).astype(jnp.float32)
    memory_heads = split_heads(memory).astype(jnp.float32)
    scores = jnp.einsum("bqhd,bkhd->bhqk", input_heads, memory_heads) * score_scale
    attn_probs = jax.nn.softmax(scores, axis=-1)
    weights = rounded(attn_probs)
    attn_mixed = jnp.einsum("bhqk,bkhd->bqhd", weights, memory_heads)
    encoded = (input_heads + attn_mixed).astype(jnp.bfloat16)
    return encoded.reshape(inputs.shape), attn_probs, weights


def encode_backward(inputs, memory, attn_probs, weights, grad_encoded):
    score_scale = HD ** -0.5
    input_heads = split_heads(inputs).astype(jnp.float32)
    memory_heads = split_heads(memory).astype(jnp.float32)
    grad_heads = split_heads(grad_encoded).astype(jnp.float32)
    grad_probs = jnp.einsum("bqhd,bkhd->bhqk", grad_heads, memory_heads)
    grad_scores = attn_probs * (grad_probs - jnp.sum(attn_probs * grad_probs, axis=-1, keepdims=True))
    grad_scores = rounded(grad_scores)
    from_scores = jnp.einsum("bhqk,bqhd->bkhd", grad_scores, input_heads) * score_scale
    from_values = jnp.einsum("bhqk,bqhd->bkhd", weights, grad_heads)
    return (from_scores + from_values).astype(jnp.bfloat16).reshape(memory.shape)


def cross_backward(queries, keys, grad_output):
    score_scale = HD ** -0.5
    query_heads = split_heads(queries).astype(jnp.float32)
    key_heads = split_heads(keys).astype(jnp.float32)
    grad_heads = split_heads(grad_output).astype(jnp.float32)
    scores = jnp.einsum("cqhd,ckhd->chqk", query_heads, key_heads) * score_scale
    attn_probs = jax.nn.softmax(scores, axis=-1)
    weights = rounded(attn_probs)
    grad_probs = jnp.einsum("cqhd,ckhd->chqk", grad_heads, key_heads)
    grad_scores = attn_probs * (grad_probs - jnp.sum(attn_probs * grad_probs, axis=-1, keepdims=True))
    grad_scores = rounded(grad_scores)
    grad_queries = (jnp.einsum("chqk,ckhd->cqhd", grad_scores, key_heads) * score_scale).astype(jnp.bfloat16)
    from_scores = jnp.einsum("chqk,cqhd->ckhd", grad_scores, query_heads) * score_scale
    from_values = jnp.einsum("chqk,cqhd->ckhd", weights, grad_heads)
    grad_keys = (from_scores + from_values).astype(jnp.bfloat16)
    return grad_queries.reshape(queries.shape), grad_keys.reshape(keys.shape)


def reference(states, projections, neighbours, owner, slot, cotangent):
    queries = jnp.dot(states, projections[0], preferred_element_type=jnp.float32).astype(jnp.bfloat16)
    memory = jnp.dot(states, projections[1], preferred_element_type=jnp.float32).astype(jnp.bfloat16)
    neigh_index = (owner * NB_DEV + slot).astype(jnp.int32).reshape(N_SEQ, NB_DEV)

    def per_shard(shard_block):
        neigh_ids, memory_rows, query_rows, grad_rows = shard_block
        inputs = neighbours[neigh_ids]
        group_memory = jnp.repeat(memory_rows, KNB, axis=0)
        encoded, attn_probs, weights = encode_forward(inputs, group_memory)
        keys = encoded.reshape(CH_DEV, KNB * NLEN, HE)
        grad_queries, grad_keys = cross_backward(query_rows, keys, grad_rows)
        grad_each = encode_backward(inputs, group_memory, attn_probs, weights, grad_keys.reshape(NB_DEV, NLEN, HE))
        summed = jnp.sum(grad_each.reshape(CH_DEV, KNB, GROUP, HE).astype(jnp.float32), axis=1)
        return grad_queries, summed.astype(jnp.bfloat16)

    shard_inputs = (
        neigh_index,
        memory.reshape(N_SEQ, CH_DEV, GROUP, HE),
        queries.reshape(N_SEQ, CH_DEV, GROUP, HE),
        cotangent.reshape(N_SEQ, CH_DEV, GROUP, HE),
    )
    grads_query, grads_memory = lax.map(per_shard, shard_inputs)
    from_queries = jnp.dot(grads_query.reshape(TOKENS, HE), projections[0].T, preferred_element_type=jnp.float32)
    from_memory = jnp.dot(grads_memory.reshape(TOKENS, HE), projections[1].T, preferred_element_type=jnp.float32)
    return (from_queries + from_memory).astype(jnp.bfloat16)
```

```python
import jax
import jax.numpy as jnp
from jax import lax
from jax.experimental import pallas as pl
from jax.experimental.pallas import tpu as pltpu
from jax.sharding import PartitionSpec as P

HD = 128
GROUP = 64
KNB = 2
CAP = 2
SCALE = HD ** (-0.5)
VMEM_LIMIT = 48 * 1024 * 1024


def swap_cores(block):
    return lax.ppermute(block, "grp", [(0, 1), (1, 0)])


def dot_nt(a, b):
    return lax.dot_general(a, b, (((1,), (1,)), ((), ())), preferred_element_type=jnp.float32)


def dot_tn(a, b):
    return lax.dot_general(a, b, (((0,), (0,)), ((), ())), preferred_element_type=jnp.float32)


def dot_nn(a, b):
    return lax.dot_general(a, b, (((1,), (0,)), ((), ())), preferred_element_type=jnp.float32)


def pick_kernel(count, last, index_ref, source_ref, out_ref):
    def step(i, carry):
        out_ref[i] = source_ref[jnp.clip(index_ref[i], 0, last)]
        return carry

    lax.fori_loop(0, count, step, 0)


def pick_blocks(index, source):
    count = index.shape[0]
    rows, columns = source.shape[1:]
    return pl.pallas_call(
        lambda *refs: pick_kernel(count, source.shape[0] - 1, *refs),
        out_shape=jax.ShapeDtypeStruct((count, rows, columns), source.dtype),
        in_specs=[
            pl.BlockSpec(memory_space=pltpu.SMEM),
            pl.BlockSpec(memory_space=pltpu.VMEM),
        ],
        out_specs=pl.BlockSpec(memory_space=pltpu.VMEM),
        compiler_params=pltpu.CompilerParams(vmem_limit_bytes=VMEM_LIMIT),
        name="pick_blocks",
    )(index, source)


def head_gradients(queries, memory, inputs, grad_out):
    scores = dot_nt(memory, inputs) * SCALE
    scores = jnp.exp(scores - jnp.max(scores, axis=0, keepdims=True))
    enc_probs = scores * (1.0 / jnp.sum(scores, axis=0, keepdims=True))
    enc_weights = enc_probs.astype(jnp.bfloat16)
    mixed = dot_tn(enc_weights, memory)
    keys = (inputs.astype(jnp.float32) + mixed).astype(jnp.bfloat16)
    scores = dot_nt(queries, keys) * SCALE
    scores = jnp.exp(scores - jnp.max(scores, axis=1, keepdims=True))
    probs = scores * (1.0 / jnp.sum(scores, axis=1, keepdims=True))
    weights = probs.astype(jnp.bfloat16)
    grad_probs = dot_nt(grad_out, keys)
    grad_scores = probs * (grad_probs - jnp.sum(probs * grad_probs, axis=1, keepdims=True))
    grad_scores = grad_scores.astype(jnp.bfloat16)
    grad_queries = dot_nn(grad_scores, keys) * SCALE
    grad_keys = dot_tn(grad_scores, queries) * SCALE + dot_tn(weights, grad_out)
    grad_keys = grad_keys.astype(jnp.bfloat16)
    grad_probs = dot_nt(memory, grad_keys)
    grad_scores = enc_probs * (grad_probs - jnp.sum(enc_probs * grad_probs, axis=0, keepdims=True))
    grad_scores = grad_scores.astype(jnp.bfloat16)
    grad_memory = dot_nn(grad_scores, inputs) * SCALE + dot_nn(enc_weights, grad_keys)
    return grad_queries.astype(jnp.bfloat16), grad_memory.astype(jnp.bfloat16)


def attend_kernel(side_ref, own_ref, other_ref, cot_ref, near_ref, far_ref, grad_own_ref, grad_other_ref):
    side = side_ref[0]
    half = near_ref.shape[1]
    first = side == 0
    for far in range(2):
        held_ref = far_ref if far else near_ref
        start = ((side + far) % 2) * half
        for low in range(0, half, HD):
            lanes = pl.ds(pl.multiple_of(start + low, HD), HD)
            own = own_ref[:, lanes]
            other = other_ref[:, lanes]
            grad_q, grad_m = head_gradients(
                jnp.where(first, own, other),
                jnp.where(first, other, own),
                held_ref[:, low : low + HD],
                cot_ref[:, lanes],
            )
            grad_own_ref[:, lanes] = jnp.where(first, grad_q, grad_m)
            grad_other_ref[:, lanes] = jnp.where(first, grad_m, grad_q)


def attend(side, own, other, cotangent, near, far):
    tokens, width = own.shape
    half = near.shape[1]
    token_spec = pl.BlockSpec((GROUP, width), lambda c, s: (c, 0))
    neigh_spec = pl.BlockSpec((KNB * near.shape[0] // (tokens // GROUP * KNB), half), lambda c, s: (c, 0))
    return pl.pallas_call(
        attend_kernel,
        grid_spec=pltpu.PrefetchScalarGridSpec(
            num_scalar_prefetch=1,
            grid=(tokens // GROUP,),
            in_specs=[token_spec] * 3 + [neigh_spec] * 2,
            out_specs=[token_spec] * 2,
        ),
        out_shape=[jax.ShapeDtypeStruct((tokens, width), jnp.bfloat16)] * 2,
        compiler_params=pltpu.CompilerParams(vmem_limit_bytes=VMEM_LIMIT),
        name="attend",
    )(side, own, other, cotangent, near, far)


def shards(states, projections, neighbours, owner, slot, cotangent):
    side = lax.axis_index("grp")
    owner_count = lax.axis_size("seq")
    tp_count = lax.axis_size("tp")
    tokens = states.shape[0] // 2
    groups = owner.shape[0]
    neigh_count = groups * KNB
    slot_count = owner_count * CAP
    owned, neigh_len, features = neighbours.shape
    half = features // 2

    target = owner.reshape(neigh_count)
    owner_slot = slot.reshape(neigh_count)
    order = jnp.arange(neigh_count)
    earlier = (target[:, None] == target[None, :]) & (order[None, :] < order[:, None])
    position = target * CAP + jnp.sum(earlier.astype(jnp.int32), axis=1)
    picked = jnp.arange(slot_count)[:, None] == position[None, :]
    labels = jnp.sum(jnp.where(picked, owner_slot[None, :], 0), axis=1).reshape(owner_count, CAP)
    labels = lax.all_to_all(labels, "seq", split_axis=0, concat_axis=0, tiled=True)

    neigh_half = lax.dynamic_slice_in_dim(neighbours, side * half, half, 2)
    outgoing = pick_blocks(labels.reshape(slot_count), neigh_half)
    incoming = lax.all_to_all(
        outgoing.reshape(owner_count, CAP, neigh_len, half), "seq", split_axis=0, concat_axis=0, tiled=True
    ).reshape(slot_count, neigh_len, half)

    rows = lax.dynamic_slice_in_dim(states, side * tokens, tokens, 0)
    gathered = lax.all_gather(rows, "tp", axis=1, tiled=True)
    own_weight = projections[0]
    other_weight = swap_cores(own_weight)
    own = jnp.dot(gathered, own_weight, preferred_element_type=jnp.float32).astype(jnp.bfloat16)
    other = jnp.dot(gathered, other_weight, preferred_element_type=jnp.float32).astype(jnp.bfloat16)

    mine = neigh_count // 2
    keep = lax.dynamic_slice_in_dim(position, side * mine, mine, 0)
    give = lax.dynamic_slice_in_dim(position, (1 - side) * mine, mine, 0)
    far = swap_cores(pick_blocks(give, incoming))
    near = pick_blocks(keep, incoming)
    grad_output = lax.dynamic_slice_in_dim(cotangent, side * tokens, tokens, 0)
    grad_own, grad_other = attend(
        side.reshape(1).astype(jnp.int32),
        own,
        other,
        grad_output,
        near.reshape(mine * neigh_len, half),
        far.reshape(mine * neigh_len, half),
    )

    width = own_weight.shape[0] // 2

    def partial_half(which):
        rows_own = own_weight[which * width : (which + 1) * width]
        rows_other = other_weight[which * width : (which + 1) * width]
        return (dot_nt(grad_own, rows_own) + dot_nt(grad_other, rows_other)).astype(jnp.bfloat16)

    partial_term = jnp.stack([partial_half(0), partial_half(1)])
    summed = lax.psum_scatter(partial_term, "tp", scatter_dimension=2, tiled=True)
    kept = lax.dynamic_index_in_dim(summed, side, 0, keepdims=False)
    given = lax.dynamic_index_in_dim(summed, 1 - side, 0, keepdims=False)
    received = swap_cores(given)
    return jnp.where(
        side == 0, jnp.concatenate([kept, received]), jnp.concatenate([received, kept])
    )


def solution(mesh):
    return jax.shard_map(
        shards,
        mesh=mesh,
        in_specs=(
            P("seq", "tp"),
            P("grp", None, "tp"),
            P("seq", None, "tp"),
            P("seq", None),
            P("seq", None),
            P("seq", "tp"),
        ),
        out_specs=P("seq", ("grp", "tp")),
        check_vma=False,
    )
```

```python
import jax
import jax.numpy as jnp
from jax import lax
from jax.experimental import pallas as pl
from jax.experimental.pallas import tpu as pltpu
from jax.sharding import PartitionSpec as P

HD = 128
GROUP = 64
KNB = 2
SCALE = HD ** (-0.5)
MIB = 1024 * 1024
BF16 = jnp.bfloat16


def dot_nt(a, b):
    return lax.dot_general(a, b, (((1,), (1,)), ((), ())), preferred_element_type=jnp.float32)


def dot_tn(a, b):
    return lax.dot_general(a, b, (((0,), (0,)), ((), ())), preferred_element_type=jnp.float32)


def dot_nn(a, b):
    return lax.dot_general(a, b, (((1,), (0,)), ((), ())), preferred_element_type=jnp.float32)


def params(mib=16):
    return pltpu.CompilerParams(vmem_limit_bytes=mib * MIB)


def whole(shape):
    return pl.BlockSpec(shape, lambda *i: (0,) * len(shape))


def glance(array):
    return pl.BlockSpec((1,) * (array.ndim - 2) + (16, HD), lambda *i: (0,) * array.ndim)


def swap_cores(block):
    return lax.ppermute(block, "grp", [(0, 1), (1, 0)])


def shift(block, step):
    count = lax.axis_size("tp")
    return lax.ppermute(block, "tp", [(i, (i + step) % count) for i in range(count)])


def swap(block, mask):
    count = lax.axis_size("tp")
    return lax.ppermute(block, "tp", [(i, i ^ mask) for i in range(count)])


TABLE = 8


def batch_of(owned):
    return 8 if owned % 8 == 0 else owned


def order_matrix(batch, parts, deep, back):
    size = batch * parts * deep
    row = lax.broadcasted_iota(jnp.int32, (size, size), 0)
    column = lax.broadcasted_iota(jnp.int32, (size, size), 1)
    travel, home = (column, row) if back else (row, column)
    where = (travel % batch) * (parts * deep) + travel // batch
    return (home == where).astype(jnp.float32).astype(BF16)


def table_rows(owner, slot, owned, half):
    batch = batch_of(owned)
    groups = owner.shape[0]
    number = KNB * lax.broadcasted_iota(jnp.int32, (groups, half), 0)
    column = lax.broadcasted_iota(jnp.int32, (groups, half), 1)
    rows = []
    for values in (slot // batch, owner * batch + slot % batch):
        row = jnp.zeros((1, half), jnp.int32)
        for k in range(KNB):
            spread = jnp.where(column == number + k, values[:, k : k + 1], 0)
            row = row + jnp.sum(spread, axis=0, keepdims=True)
        rows.append(row)
    which = lax.broadcasted_iota(jnp.int32, (TABLE, half), 0)
    table = jnp.where(which == 0, rows[0], jnp.where(which == 1, rows[1], 0))
    return table.astype(jnp.float32).astype(BF16)


def pack_kernel(batch, place_ref, owner_ref, slot_ref, neigh_ref, out_ref):
    owned, rows, half = neigh_ref.shape
    parts = out_ref.shape[0]
    deep = rows // parts
    chooser = order_matrix(batch, parts, deep, False)
    for first in range(0, owned, batch):
        block = neigh_ref[first : first + batch].reshape(batch * rows, half)
        moved = dot_nn(chooser, block).astype(BF16).reshape(parts, deep * batch, half)
        out_ref[:, first * deep : (first + batch) * deep] = moved
    table = table_rows(owner_ref[...], slot_ref[...], owned, half)
    out_ref[:, owned * deep :] = jnp.broadcast_to(table[None], (parts, TABLE, half))


def pack_rows(place, owner, slot, neighbours, parts):
    owned, rows, features = neighbours.shape
    half = features // 2
    message = owned * (rows // parts) + TABLE
    batch = batch_of(owned)
    return pl.pallas_call(
        lambda *refs: pack_kernel(batch, *refs),
        grid_spec=pltpu.PrefetchScalarGridSpec(
            num_scalar_prefetch=1,
            grid=(1,),
            in_specs=[whole(owner.shape)] * 2
            + [pl.BlockSpec((owned, rows, half), lambda i, s: (0, 0, s[0]))],
            out_specs=whole((parts, message, half)),
        ),
        out_shape=jax.ShapeDtypeStruct((parts, message, half), BF16),
        compiler_params=params(60),
        name="pack_rows",
    )(place, owner, slot, neighbours)


def route_kernel(owned, batch, held_ref, *refs):
    out_ref = refs[-1]
    owners, message, half = held_ref.shape
    deep = (message - TABLE) // owned
    total = owners * owned
    table = held_ref[:, owned * deep :, :].astype(jnp.float32).reshape(owners * TABLE, half)[:, :HD].T
    held = []
    for first in range(0, owned, batch):
        block = held_ref[:, first * deep : (first + batch) * deep].astype(jnp.float32)
        rows = [block[:, r * batch : (r + 1) * batch].reshape(owners * batch, half) for r in range(deep)]
        held.append(jnp.concatenate(rows, axis=1).astype(BF16))
    held = jnp.concatenate(held, axis=0)
    columns = lax.broadcasted_iota(jnp.int32, (owned, total), 1).astype(jnp.float32)
    per_dot = min(8, owners)
    for start in range(0, owners, per_dot):
        choose = []
        for s in range(start, start + per_dot):
            high = table[:owned, s * TABLE : s * TABLE + 1]
            low = table[:owned, s * TABLE + 1 : s * TABLE + 2]
            choose.append((high * float(owners * batch) + low == columns).astype(jnp.float32))
        moved = dot_nn(jnp.concatenate(choose, axis=0).astype(BF16), held).reshape(per_dot, owned, deep * half)
        for first in range(0, owned, batch):
            rows = [moved[:, first : first + batch, r * half : (r + 1) * half] for r in range(deep)]
            place = pl.ds(first * deep, batch * deep)
            out_ref[start : start + per_dot, place] = jnp.concatenate(rows, axis=1).astype(BF16)


def route_rows(held, owned, after):
    owners, message, half = held.shape
    batch = batch_of(owned)
    out_shape = (owners, message - TABLE, half)
    return pl.pallas_call(
        lambda *refs: route_kernel(owned, batch, *refs),
        grid=(1,),
        out_shape=jax.ShapeDtypeStruct(out_shape, BF16),
        in_specs=[whole(held.shape)] + [glance(x) for x in after],
        out_specs=whole(out_shape),
        compiler_params=params(),
        name="route_rows",
    )(held, *after)


def unpack_kernel(owned, batch, place_ref, arrived_ref, *refs):
    keep_ref, give_ref = refs[-2:]
    parts, message, half = arrived_ref.shape
    deep = message // owned
    rows = parts * deep
    chooser = order_matrix(batch, parts, deep, True)
    mine = owned // 2
    side = place_ref[0]
    for first in range(0, owned, batch):
        block = arrived_ref[:, first * deep : (first + batch) * deep].reshape(batch * rows, half)
        sorted_rows = dot_nn(chooser, block).astype(BF16)
        for n in range(first, first + batch, KNB):
            group = sorted_rows[(n - first) * rows : (n - first + KNB) * rows]
            place = pl.ds(n % mine * rows, KNB * rows)

            @pl.when(side == n // mine)
            def _():
                keep_ref[place] = group

            @pl.when(side != n // mine)
            def _():
                give_ref[place] = group


def unpack_rows(place, arrived, owned, rows, after):
    parts, message, half = arrived.shape
    batch = batch_of(owned)
    out_shape = (owned // 2 * rows, half)
    return pl.pallas_call(
        lambda *refs: unpack_kernel(owned, batch, *refs),
        grid_spec=pltpu.PrefetchScalarGridSpec(
            num_scalar_prefetch=1,
            grid=(1,),
            in_specs=[whole(arrived.shape)] + [glance(x) for x in after],
            out_specs=[whole(out_shape)] * 2,
        ),
        out_shape=[jax.ShapeDtypeStruct(out_shape, BF16)] * 2,
        compiler_params=params(),
        name="unpack_rows",
    )(place, arrived, *after)


def project_kernel(place_ref, *refs):
    blocks, (own_w, other_w, own_out, other_out) = refs[:-4], refs[-4:]
    step = pl.program_id(0)
    for k, block_ref in enumerate(blocks):

        @pl.when(step == k)
        def _():
            block = block_ref[...]
            own = dot_nn(block, own_w[...])
            other = dot_nn(block, other_w[...])
            own_out[...] = own if k == 0 else own_out[...] + own
            other_out[...] = other if k == 0 else other_out[...] + other


def project_last_kernel(place_ref, *refs):
    pieces, (own_in, other_in, own_w, other_w, own_out, other_out) = refs[:-6], refs[-6:]
    first = 0
    for piece_ref in pieces:
        piece = piece_ref[...]
        rows = slice(first, first + piece.shape[0])
        own_out[rows] = (own_in[rows] + dot_nn(piece, own_w[...])).astype(BF16)
        other_out[rows] = (other_in[rows] + dot_nn(piece, other_w[...])).astype(BF16)
        first += piece.shape[0]


def project(place, masks, blocks, own_weight, other_weight, sums=None):
    depth = blocks[0].shape[1]
    width = own_weight.shape[1]
    final = sums is not None
    tokens = sum(x.shape[0] for x in blocks) if final else blocks[0].shape[0]

    def mask_of(k):
        return sum(jnp.where(k == i, m, 0) for i, m in enumerate(masks))

    weight_spec = pl.BlockSpec((depth, width), lambda k, s: (s[1] ^ mask_of(k), 0))
    out_spec = whole((tokens, width))
    shape = jax.ShapeDtypeStruct((tokens, width), BF16 if final else jnp.float32)
    return pl.pallas_call(
        project_last_kernel if final else project_kernel,
        grid_spec=pltpu.PrefetchScalarGridSpec(
            num_scalar_prefetch=1,
            grid=(len(masks),),
            in_specs=[whole(x.shape) for x in blocks] + [out_spec] * (2 * final) + [weight_spec] * 2,
            out_specs=[out_spec] * 2,
        ),
        out_shape=[shape, shape],
        compiler_params=params(60),
        name="project",
    )(place, *blocks, *(sums or ()), own_weight, other_weight)


def heads_gradients(items):
    queries, memory, inputs, grad_out = zip(*items)
    count = range(len(items))
    scores = [dot_nt(memory[i], inputs[i]) * SCALE for i in count]
    scores = [jnp.exp(s - jnp.max(s, axis=0, keepdims=True)) for s in scores]
    enc_probs = [s * (1.0 / jnp.sum(s, axis=0, keepdims=True)) for s in scores]
    enc_weights = [p.astype(BF16) for p in enc_probs]
    mixed = [dot_tn(enc_weights[i], memory[i]) for i in count]
    keys = [(inputs[i].astype(jnp.float32) + mixed[i]).astype(BF16) for i in count]
    scores = [dot_nt(queries[i], keys[i]) * SCALE for i in count]
    grad_probs = [dot_nt(grad_out[i], keys[i]) for i in count]
    scores = [jnp.exp(s - jnp.max(s, axis=1, keepdims=True)) for s in scores]
    probs = [s * (1.0 / jnp.sum(s, axis=1, keepdims=True)) for s in scores]
    weights = [p.astype(BF16) for p in probs]
    from_values = [dot_tn(weights[i], grad_out[i]) for i in count]
    grad_scores = [p * (g - jnp.sum(p * g, axis=1, keepdims=True)) for p, g in zip(probs, grad_probs)]
    grad_scores = [g.astype(BF16) for g in grad_scores]
    grad_keys = [dot_tn(grad_scores[i], queries[i]) * SCALE + from_values[i] for i in count]
    grad_keys = [g.astype(BF16) for g in grad_keys]
    grad_queries = [(dot_nn(grad_scores[i], keys[i]) * SCALE).astype(BF16) for i in count]
    grad_probs = [dot_nt(memory[i], grad_keys[i]) for i in count]
    from_values = [dot_nn(enc_weights[i], grad_keys[i]) for i in count]
    grad_scores = [p * (g - jnp.sum(p * g, axis=0, keepdims=True)) for p, g in zip(enc_probs, grad_probs)]
    grad_scores = [g.astype(BF16) for g in grad_scores]
    grad_memory = [(dot_nn(grad_scores[i], inputs[i]) * SCALE + from_values[i]).astype(BF16) for i in count]
    return grad_queries, grad_memory


def attend_kernel(
    tp_count, far_step, place_ref, own_ref, other_ref, cot_ref, near_ref, far_ref, own_hbm, other_hbm,
    grad_own_ref, grad_other_ref, low_ref, high_ref, weights, arrived,
):
    step = pl.program_id(0)
    side = place_ref[0]
    columns = weights.shape[1]
    target = (place_ref[1] + far_step) % tp_count
    copies = [
        pltpu.make_async_copy(
            hbm.at[pl.ds(pl.multiple_of((target + core * tp_count) * columns, columns), columns)],
            weights.at[2 * core + i],
            arrived.at[2 * core + i],
        )
        for core in range(2)
        for i, hbm in enumerate((own_hbm, other_hbm))
    ]

    @pl.when(step == 0)
    def _():
        for copy in copies:
            copy.start()

    half = near_ref.shape[1]
    first = side == 0
    tokens = own_ref.shape[0]
    groups = tokens // GROUP
    keys = near_ref.shape[0] // groups
    items, spots = [], []
    for c in range(groups):
        rows = slice(c * GROUP, (c + 1) * GROUP)
        place = pl.ds(pl.multiple_of(step * tokens + c * GROUP, GROUP), GROUP)
        for far, held_ref in enumerate((near_ref, far_ref)):
            start = ((side + far) % 2) * half
            for low in range(0, half, HD):
                lanes = pl.ds(pl.multiple_of(start + low, HD), HD)
                own = own_ref[rows, lanes]
                other = other_ref[rows, lanes]
                items.append(
                    (
                        jnp.where(first, own, other),
                        jnp.where(first, other, own),
                        held_ref[c * keys : (c + 1) * keys, low : low + HD],
                        cot_ref[rows, lanes],
                    )
                )
                spots.append((place, lanes))
    grad_queries, grad_memory = heads_gradients(items)
    for spot, grad_q, grad_m in zip(spots, grad_queries, grad_memory):
        grad_own_ref[spot] = jnp.where(first, grad_q, grad_m)
        grad_other_ref[spot] = jnp.where(first, grad_m, grad_q)

    @pl.when(step == pl.num_programs(0) - 1)
    def _():
        for copy in copies:
            copy.wait()
        low_rows = low_ref.shape[0]
        grad_own, grad_other = grad_own_ref[...], grad_other_ref[...]
        for core in range(2):
            term = dot_nt(grad_own, weights[2 * core]) + dot_nt(grad_other, weights[2 * core + 1])
            term = term.astype(BF16)
            low_ref[:, core * columns : (core + 1) * columns] = term[:low_rows]
            high_ref[:, core * columns : (core + 1) * columns] = term[low_rows:]


def attend(place, own, other, cotangent, near, far, own_weight, other_weight):
    tokens, width = own.shape
    rows, half = near.shape
    groups = tokens // GROUP
    steps = groups // 3 if groups % 3 == 0 else groups
    tp_count = lax.axis_size("tp")
    columns = own_weight.shape[0] // (2 * tp_count)
    token_spec = pl.BlockSpec((tokens // steps, width), lambda c, s: (c, 0))
    cot_spec = pl.BlockSpec((tokens // steps, width), lambda c, s: (s[0] * steps + c, 0))
    neigh_spec = pl.BlockSpec((rows // steps, half), lambda c, s: (c, 0))
    outs = [(tokens, width)] * 2 + [(tokens // 2, 2 * columns)] * 2
    return pl.pallas_call(
        lambda *refs: attend_kernel(tp_count, tp_count // 2, *refs),
        grid_spec=pltpu.PrefetchScalarGridSpec(
            num_scalar_prefetch=1,
            grid=(steps,),
            in_specs=[token_spec] * 2 + [cot_spec] + [neigh_spec] * 2 + [pl.BlockSpec(memory_space=pl.ANY)] * 2,
            out_specs=[whole(shape) for shape in outs],
            scratch_shapes=[pltpu.VMEM((4, columns, width), BF16), pltpu.SemaphoreType.DMA((4,))],
        ),
        out_shape=[jax.ShapeDtypeStruct(shape, BF16) for shape in outs],
        compiler_params=params(57),
        name="attend",
    )(place, own, other, cotangent, near, far, own_weight, other_weight)


def partial_kernel(steps, place_ref, own_ref, other_ref, own_a, own_b, other_a, other_b, *out_refs):
    columns = own_a.shape[0]
    low_rows = own_ref.shape[0] // 2
    for i in range(len(steps)):

        @pl.when(pl.program_id(0) == i)
        def _():
            own, other = own_ref[...], other_ref[...]
            for core, weights in enumerate(((own_a, other_a), (own_b, other_b))):
                term = dot_nt(own, weights[0][...]) + dot_nt(other, weights[1][...])
                term = term.astype(BF16)
                place = slice(core * columns, (core + 1) * columns)
                out_refs[2 * i][:, place] = term[:low_rows]
                out_refs[2 * i + 1][:, place] = term[low_rows:]


def partial_terms(place, steps, grad_own, grad_other, own_weight, other_weight):
    tokens, width = grad_own.shape
    tp_count = lax.axis_size("tp")
    columns = own_weight.shape[0] // (2 * tp_count)

    def weight_spec(core):
        def index(i, s):
            step = sum(jnp.where(i == u, step, 0) for u, step in enumerate(steps))
            return ((s[1] + step) % tp_count + core * tp_count, 0)

        return pl.BlockSpec((columns, width), index)

    shape = (tokens // 2, 2 * columns)
    return pl.pallas_call(
        lambda *refs: partial_kernel(steps, *refs),
        grid_spec=pltpu.PrefetchScalarGridSpec(
            num_scalar_prefetch=1,
            grid=(len(steps),),
            in_specs=[whole((tokens, width))] * 2 + [weight_spec(0), weight_spec(1)] * 2,
            out_specs=[whole(shape)] * (2 * len(steps)),
        ),
        out_shape=[jax.ShapeDtypeStruct(shape, BF16)] * (2 * len(steps)),
        compiler_params=params(57),
        name="partial_terms",
    )(place, grad_own, grad_other, own_weight, own_weight, other_weight, other_weight)


def add_terms(a, b):
    return (a.astype(jnp.float32) + b.astype(jnp.float32)).astype(BF16)


def scatter_ring(place, across_low, across_high, *operands):
    if lax.axis_size("tp") == 2:
        own_low, own_high = partial_terms(place, (0,), *operands)
        return [own_low, shift(across_low, 1)], [own_high, shift(across_high, 1)]
    rising = shift(across_low, 1)
    falling = shift(across_high, -1)
    up_low, up_high, down_low, down_high, own_low, own_high = partial_terms(place, (1, 3, 0), *operands)
    up_high = shift(up_high, 1)
    down_low = shift(down_low, -1)
    up_low = shift(add_terms(up_low, rising), 1)
    down_high = shift(add_terms(down_high, falling), -1)
    return [own_low, down_low, up_low], [own_high, up_high, down_high]


def sum_terms(terms):
    return sum(term[...].astype(jnp.float32) for term in terms).astype(BF16)


def give_kernel(place_ref, *refs):
    terms, out_ref = refs[:-1], refs[-1]
    count, rows = len(terms) // 2, terms[0].shape[0]
    out_ref[:rows] = sum_terms(terms[:count])
    out_ref[rows:] = sum_terms(terms[count:])


def keep_kernel(place_ref, *refs):
    terms, received_ref, out_ref = refs[:-2], refs[-2], refs[-1]
    count, rows = len(terms) // 2, terms[0].shape[0]
    side = place_ref[0]
    mine = pl.multiple_of(side * 2 * rows, 2 * rows)
    other = pl.multiple_of((1 - side) * 2 * rows, 2 * rows)
    out_ref[pl.ds(mine, rows)] = sum_terms(terms[:count])
    out_ref[pl.ds(mine + rows, rows)] = sum_terms(terms[count:])
    out_ref[pl.ds(other, 2 * rows)] = received_ref[...]


def sum_columns(place, lows, highs, received=None):
    rows, columns = lows[0].shape[0], lows[0].shape[1] // 2
    give = received is None
    extra = [] if give else [received]
    spec = pl.BlockSpec((rows, columns), lambda i, s: (0, 1 - s[0] if give else s[0]))
    out_shape = ((2 if give else 4) * rows, columns)
    return pl.pallas_call(
        give_kernel if give else keep_kernel,
        grid_spec=pltpu.PrefetchScalarGridSpec(
            num_scalar_prefetch=1,
            grid=(1,),
            in_specs=[spec] * len(lows + highs) + [whole(x.shape) for x in extra],
            out_specs=whole(out_shape),
        ),
        out_shape=jax.ShapeDtypeStruct(out_shape, BF16),
        compiler_params=params(),
        name="sum_columns",
    )(place, *lows, *highs, *extra)


def shards(states, projections, neighbours, owner, slot, cotangent):
    side = lax.axis_index("grp").astype(jnp.int32)
    place = jnp.stack([side, lax.axis_index("tp").astype(jnp.int32)])
    shards_ = lax.axis_size("seq")
    tp_count = lax.axis_size("tp")
    tokens = states.shape[0] // 2
    owned, rows, features = neighbours.shape

    held = lax.dynamic_slice_in_dim(states, side * tokens, tokens, 0)
    if tp_count == 2:
        blocks, masks, last = [held], [0], [swap(held, 1)]
    else:
        low = tokens // 2
        blocks, masks = [held, swap(held, 1), swap(held, 3)], [0, 1, 3]
        last = [swap(blocks[2][:low], 1), swap(blocks[1][low:], 3)]
    own_weight = projections[0]
    other_weight = swap_cores(own_weight)
    packed = pack_rows(place, owner, slot, neighbours, shards_)
    parts = lax.all_to_all(packed, "seq", split_axis=0, concat_axis=0, tiled=True)
    routed = route_rows(parts, owned, [block[:16, :HD] for block in blocks[1:]])
    arrived = lax.all_to_all(routed, "seq", split_axis=0, concat_axis=0, tiled=True)

    sums = project(place, masks, blocks, own_weight, other_weight)
    own, other = project(place, [tp_count // 2], last, own_weight, other_weight, sums)
    near, give = unpack_rows(place, arrived, owned, rows, [own[:16, :HD]])
    far = swap_cores(give)
    grad_own, grad_other, across_low, across_high = attend(
        place, own, other, cotangent, near, far, own_weight, other_weight
    )
    lows, highs = scatter_ring(place, across_low, across_high, grad_own, grad_other, own_weight, other_weight)

    received = swap_cores(sum_columns(place, lows, highs))
    return sum_columns(place, lows, highs, received)


def solution(mesh):
    return jax.shard_map(
        shards,
        mesh=mesh,
        in_specs=(
            P("seq", "tp"),
            P("grp", None, "tp"),
            P("seq", None, "tp"),
            P("seq", None),
            P("seq", None),
            P("seq", "tp"),
        ),
        out_specs=P("seq", ("grp", "tp")),
        check_vma=False,
    )
```

```python
import jax
import jax.numpy as jnp
from jax import lax
from jax.experimental import pallas as pl
from jax.experimental.pallas import tpu as pltpu
from jax.sharding import PartitionSpec as P

HD = 128
GROUP = 64
KNB = 2
SCALE = HD ** (-0.5)
MIB = 1024 * 1024
BF16 = jnp.bfloat16


def dot_nt(a, b):
    return lax.dot_general(a, b, (((1,), (1,)), ((), ())), preferred_element_type=jnp.float32)


def dot_tn(a, b):
    return lax.dot_general(a, b, (((0,), (0,)), ((), ())), preferred_element_type=jnp.float32)


def dot_nn(a, b):
    return lax.dot_general(a, b, (((1,), (0,)), ((), ())), preferred_element_type=jnp.float32)


def params(mib=16):
    return pltpu.CompilerParams(vmem_limit_bytes=mib * MIB)


def cost(us):
    return pl.CostEstimate(flops=int(us * 1e9), bytes_accessed=int(us * 1e6), transcendentals=0)


def whole(shape):
    return pl.BlockSpec(shape, lambda *i: (0,) * len(shape))


def glance(array):
    return pl.BlockSpec((1,) * (array.ndim - 2) + (16, HD), lambda *i: (0,) * array.ndim)


def swap_cores(block):
    return lax.ppermute(block, "grp", [(0, 1), (1, 0)])


def shift(block, step):
    count = lax.axis_size("tp")
    return lax.ppermute(block, "tp", [(i, (i + step) % count) for i in range(count)])


def swap(block, mask):
    count = lax.axis_size("tp")
    return lax.ppermute(block, "tp", [(i, i ^ mask) for i in range(count)])


TABLE = 8


def batch_of(owned):
    return 8 if owned % 8 == 0 else owned


def order_matrix(batch, parts, deep, back):
    size = batch * parts * deep
    row = lax.broadcasted_iota(jnp.int32, (size, size), 0)
    column = lax.broadcasted_iota(jnp.int32, (size, size), 1)
    travel, home = (column, row) if back else (row, column)
    where = (travel % batch) * (parts * deep) + travel // batch
    return (home == where).astype(jnp.float32).astype(BF16)


def table_rows(owner, slot, owned, half):
    batch = batch_of(owned)
    groups = owner.shape[0]
    number = KNB * lax.broadcasted_iota(jnp.int32, (groups, half), 0)
    column = lax.broadcasted_iota(jnp.int32, (groups, half), 1)
    rows = []
    for values in (slot // batch, owner * batch + slot % batch):
        row = jnp.zeros((1, half), jnp.int32)
        for k in range(KNB):
            spread = jnp.where(column == number + k, values[:, k : k + 1], 0)
            row = row + jnp.sum(spread, axis=0, keepdims=True)
        rows.append(row)
    which = lax.broadcasted_iota(jnp.int32, (TABLE, half), 0)
    table = jnp.where(which == 0, rows[0], jnp.where(which == 1, rows[1], 0))
    return table.astype(jnp.float32).astype(BF16)


def pack_kernel(batch, place_ref, owner_ref, slot_ref, neigh_ref, out_ref):
    owned, rows, half = neigh_ref.shape
    parts = out_ref.shape[0]
    deep = rows // parts
    chooser = order_matrix(batch, parts, deep, False)
    for first in range(0, owned, batch):
        block = neigh_ref[first : first + batch].reshape(batch * rows, half)
        moved = dot_nn(chooser, block).astype(BF16).reshape(parts, deep * batch, half)
        out_ref[:, first * deep : (first + batch) * deep] = moved
    table = table_rows(owner_ref[...], slot_ref[...], owned, half)
    out_ref[:, owned * deep :] = jnp.broadcast_to(table[None], (parts, TABLE, half))


def pack_rows(place, owner, slot, neighbours, parts):
    owned, rows, features = neighbours.shape
    half = features // 2
    message = owned * (rows // parts) + TABLE
    batch = batch_of(owned)
    return pl.pallas_call(
        lambda *refs: pack_kernel(batch, *refs),
        grid_spec=pltpu.PrefetchScalarGridSpec(
            num_scalar_prefetch=1,
            grid=(1,),
            in_specs=[whole(owner.shape)] * 2
            + [pl.BlockSpec((owned, rows, half), lambda i, s: (0, 0, s[0]))],
            out_specs=whole((parts, message, half)),
        ),
        out_shape=jax.ShapeDtypeStruct((parts, message, half), BF16),
        compiler_params=params(60),
        cost_estimate=cost(3),
        name="pack_rows",
    )(place, owner, slot, neighbours)


def route_kernel(owned, batch, held_ref, *refs):
    out_ref = refs[-1]
    owners, message, half = held_ref.shape
    deep = (message - TABLE) // owned
    total = owners * owned
    table = held_ref[:, owned * deep :, :].astype(jnp.float32).reshape(owners * TABLE, half)[:, :HD].T
    held = []
    for first in range(0, owned, batch):
        block = held_ref[:, first * deep : (first + batch) * deep].astype(jnp.float32)
        rows = [block[:, r * batch : (r + 1) * batch].reshape(owners * batch, half) for r in range(deep)]
        held.append(jnp.concatenate(rows, axis=1).astype(BF16))
    held = jnp.concatenate(held, axis=0)
    columns = lax.broadcasted_iota(jnp.int32, (owned, total), 1).astype(jnp.float32)
    per_dot = min(8, owners)
    for start in range(0, owners, per_dot):
        choose = []
        for s in range(start, start + per_dot):
            high = table[:owned, s * TABLE : s * TABLE + 1]
            low = table[:owned, s * TABLE + 1 : s * TABLE + 2]
            choose.append((high * float(owners * batch) + low == columns).astype(jnp.float32))
        moved = dot_nn(jnp.concatenate(choose, axis=0).astype(BF16), held).reshape(per_dot, owned, deep * half)
        for first in range(0, owned, batch):
            rows = [moved[:, first : first + batch, r * half : (r + 1) * half] for r in range(deep)]
            place = pl.ds(first * deep, batch * deep)
            out_ref[start : start + per_dot, place] = jnp.concatenate(rows, axis=1).astype(BF16)


def route_rows(held, owned, after):
    owners, message, half = held.shape
    batch = batch_of(owned)
    out_shape = (owners, message - TABLE, half)
    return pl.pallas_call(
        lambda *refs: route_kernel(owned, batch, *refs),
        grid=(1,),
        out_shape=jax.ShapeDtypeStruct(out_shape, BF16),
        in_specs=[whole(held.shape)] + [glance(x) for x in after],
        out_specs=whole(out_shape),
        compiler_params=params(16),
        cost_estimate=cost(2),
        name="route_rows",
    )(held, *after)


def unpack_kernel(owned, batch, place_ref, arrived_ref, *refs):
    keep_ref, give_ref = refs[-2:]
    parts, message, half = arrived_ref.shape
    deep = message // owned
    rows = parts * deep
    chooser = order_matrix(batch, parts, deep, True)
    mine = owned // 2
    side = place_ref[0]
    for first in range(0, owned, batch):
        block = arrived_ref[:, first * deep : (first + batch) * deep].reshape(batch * rows, half)
        sorted_rows = dot_nn(chooser, block).astype(BF16)
        for n in range(first, first + batch, KNB):
            group = sorted_rows[(n - first) * rows : (n - first + KNB) * rows]
            place = pl.ds(n % mine * rows, KNB * rows)

            @pl.when(side == n // mine)
            def _():
                keep_ref[place] = group

            @pl.when(side != n // mine)
            def _():
                give_ref[place] = group


def unpack_rows(place, arrived, owned, rows, after):
    parts, message, half = arrived.shape
    batch = batch_of(owned)
    out_shape = (owned // 2 * rows, half)
    return pl.pallas_call(
        lambda *refs: unpack_kernel(owned, batch, *refs),
        grid_spec=pltpu.PrefetchScalarGridSpec(
            num_scalar_prefetch=1,
            grid=(1,),
            in_specs=[whole(arrived.shape)] + [glance(x) for x in after],
            out_specs=[whole(out_shape)] * 2,
        ),
        out_shape=[jax.ShapeDtypeStruct(out_shape, BF16)] * 2,
        compiler_params=params(16),
        cost_estimate=cost(2),
        name="unpack_rows",
    )(place, arrived, *after)


def project_kernel(place_ref, *refs):
    blocks, (own_w, other_w, own_out, other_out) = refs[:-4], refs[-4:]
    step = pl.program_id(0)
    for k, block_ref in enumerate(blocks):

        @pl.when(step == k)
        def _():
            block = block_ref[...]
            own = dot_nn(block, own_w[...])
            other = dot_nn(block, other_w[...])
            own_out[...] = own if k == 0 else own_out[...] + own
            other_out[...] = other if k == 0 else other_out[...] + other


def project_last_kernel(place_ref, *refs):
    pieces, (own_in, other_in, own_w, other_w, own_out, other_out) = refs[:-6], refs[-6:]
    first = 0
    for piece_ref in pieces:
        piece = piece_ref[...]
        rows = slice(first, first + piece.shape[0])
        own_out[rows] = (own_in[rows] + dot_nn(piece, own_w[...])).astype(BF16)
        other_out[rows] = (other_in[rows] + dot_nn(piece, other_w[...])).astype(BF16)
        first += piece.shape[0]


def project(place, masks, blocks, own_weight, other_weight, sums=None):
    depth = blocks[0].shape[1]
    width = own_weight.shape[1]
    final = sums is not None
    tokens = sum(x.shape[0] for x in blocks) if final else blocks[0].shape[0]

    def mask_of(k):
        return sum(jnp.where(k == i, m, 0) for i, m in enumerate(masks))

    weight_spec = pl.BlockSpec((depth, width), lambda k, s: (s[1] ^ mask_of(k), 0))
    out_spec = whole((tokens, width))
    shape = jax.ShapeDtypeStruct((tokens, width), BF16 if final else jnp.float32)
    return pl.pallas_call(
        project_last_kernel if final else project_kernel,
        grid_spec=pltpu.PrefetchScalarGridSpec(
            num_scalar_prefetch=1,
            grid=(len(masks),),
            in_specs=[whole(x.shape) for x in blocks] + [out_spec] * (2 * final) + [weight_spec] * 2,
            out_specs=[out_spec] * 2,
        ),
        out_shape=[shape, shape],
        compiler_params=params(60),
        cost_estimate=cost(2.5 * len(masks)),
        name="project",
    )(place, *blocks, *(sums or ()), own_weight, other_weight)


def heads_gradients(items):
    queries, memory, inputs, grad_out = zip(*items)
    count = range(len(items))
    scores = [dot_nt(memory[i], inputs[i]) * SCALE for i in count]
    scores = [jnp.exp(s - jnp.max(s, axis=0, keepdims=True)) for s in scores]
    enc_probs = [s * (1.0 / jnp.sum(s, axis=0, keepdims=True)) for s in scores]
    enc_weights = [p.astype(BF16) for p in enc_probs]
    mixed = [dot_tn(enc_weights[i], memory[i]) for i in count]
    keys = [(inputs[i].astype(jnp.float32) + mixed[i]).astype(BF16) for i in count]
    scores = [dot_nt(queries[i], keys[i]) * SCALE for i in count]
    grad_probs = [dot_nt(grad_out[i], keys[i]) for i in count]
    scores = [jnp.exp(s - jnp.max(s, axis=1, keepdims=True)) for s in scores]
    probs = [s * (1.0 / jnp.sum(s, axis=1, keepdims=True)) for s in scores]
    weights = [p.astype(BF16) for p in probs]
    from_values = [dot_tn(weights[i], grad_out[i]) for i in count]
    grad_scores = [p * (g - jnp.sum(p * g, axis=1, keepdims=True)) for p, g in zip(probs, grad_probs)]
    grad_scores = [g.astype(BF16) for g in grad_scores]
    grad_keys = [dot_tn(grad_scores[i], queries[i]) * SCALE + from_values[i] for i in count]
    grad_keys = [g.astype(BF16) for g in grad_keys]
    grad_queries = [(dot_nn(grad_scores[i], keys[i]) * SCALE).astype(BF16) for i in count]
    grad_probs = [dot_nt(memory[i], grad_keys[i]) for i in count]
    from_values = [dot_nn(enc_weights[i], grad_keys[i]) for i in count]
    grad_scores = [p * (g - jnp.sum(p * g, axis=0, keepdims=True)) for p, g in zip(enc_probs, grad_probs)]
    grad_scores = [g.astype(BF16) for g in grad_scores]
    grad_memory = [(dot_nn(grad_scores[i], inputs[i]) * SCALE + from_values[i]).astype(BF16) for i in count]
    return grad_queries, grad_memory


def attend_kernel(
    tp_count, far_step, place_ref, own_ref, other_ref, cot_ref, near_ref, far_ref, own_hbm, other_hbm,
    grad_own_ref, grad_other_ref, low_ref, high_ref, weights, arrived,
):
    step = pl.program_id(0)
    side = place_ref[0]
    columns = weights.shape[1]
    target = (place_ref[1] + far_step) % tp_count
    copies = [
        pltpu.make_async_copy(
            hbm.at[pl.ds(pl.multiple_of((target + core * tp_count) * columns, columns), columns)],
            weights.at[2 * core + i],
            arrived.at[2 * core + i],
        )
        for core in range(2)
        for i, hbm in enumerate((own_hbm, other_hbm))
    ]

    @pl.when(step == 0)
    def _():
        for copy in copies:
            copy.start()

    half = near_ref.shape[1]
    first = side == 0
    tokens = own_ref.shape[0]
    groups = tokens // GROUP
    keys = near_ref.shape[0] // groups
    items, spots = [], []
    for c in range(groups):
        rows = slice(c * GROUP, (c + 1) * GROUP)
        place = pl.ds(pl.multiple_of(step * tokens + c * GROUP, GROUP), GROUP)
        for far, held_ref in enumerate((near_ref, far_ref)):
            start = ((side + far) % 2) * half
            for low in range(0, half, HD):
                lanes = pl.ds(pl.multiple_of(start + low, HD), HD)
                own = own_ref[rows, lanes]
                other = other_ref[rows, lanes]
                items.append(
                    (
                        jnp.where(first, own, other),
                        jnp.where(first, other, own),
                        held_ref[c * keys : (c + 1) * keys, low : low + HD],
                        cot_ref[rows, lanes],
                    )
                )
                spots.append((place, lanes))
    grad_queries, grad_memory = heads_gradients(items)
    for spot, grad_q, grad_m in zip(spots, grad_queries, grad_memory):
        grad_own_ref[spot] = jnp.where(first, grad_q, grad_m)
        grad_other_ref[spot] = jnp.where(first, grad_m, grad_q)

    @pl.when(step == pl.num_programs(0) - 1)
    def _():
        for copy in copies:
            copy.wait()
        low_rows = low_ref.shape[0]
        grad_own, grad_other = grad_own_ref[...], grad_other_ref[...]
        for core in range(2):
            term = dot_nt(grad_own, weights[2 * core]) + dot_nt(grad_other, weights[2 * core + 1])
            term = term.astype(BF16)
            low_ref[:, core * columns : (core + 1) * columns] = term[:low_rows]
            high_ref[:, core * columns : (core + 1) * columns] = term[low_rows:]


def attend(place, own, other, cotangent, near, far, own_weight, other_weight):
    tokens, width = own.shape
    rows, half = near.shape
    groups = tokens // GROUP
    steps = groups // 3 if groups % 3 == 0 else groups
    tp_count = lax.axis_size("tp")
    columns = own_weight.shape[0] // (2 * tp_count)
    token_spec = pl.BlockSpec((tokens // steps, width), lambda c, s: (c, 0))
    cot_spec = pl.BlockSpec((tokens // steps, width), lambda c, s: (s[0] * steps + c, 0))
    neigh_spec = pl.BlockSpec((rows // steps, half), lambda c, s: (c, 0))
    outs = [(tokens, width)] * 2 + [(tokens // 2, 2 * columns)] * 2
    return pl.pallas_call(
        lambda *refs: attend_kernel(tp_count, tp_count // 2, *refs),
        grid_spec=pltpu.PrefetchScalarGridSpec(
            num_scalar_prefetch=1,
            grid=(steps,),
            in_specs=[token_spec] * 2 + [cot_spec] + [neigh_spec] * 2 + [pl.BlockSpec(memory_space=pl.ANY)] * 2,
            out_specs=[whole(shape) for shape in outs],
            scratch_shapes=[pltpu.VMEM((4, columns, width), BF16), pltpu.SemaphoreType.DMA((4,))],
        ),
        out_shape=[jax.ShapeDtypeStruct(shape, BF16) for shape in outs],
        compiler_params=params(16),
        cost_estimate=cost(8),
        name="attend",
    )(place, own, other, cotangent, near, far, own_weight, other_weight)


def partial_kernel(steps, place_ref, own_ref, other_ref, own_a, own_b, other_a, other_b, *refs):
    out_refs = refs[-2 * len(steps) :]
    columns = own_a.shape[0]
    low_rows = own_ref.shape[0] // 2
    for i in range(len(steps)):

        @pl.when(pl.program_id(0) == i)
        def _():
            own, other = own_ref[...], other_ref[...]
            for core, weights in enumerate(((own_a, other_a), (own_b, other_b))):
                term = dot_nt(own, weights[0][...]) + dot_nt(other, weights[1][...])
                term = term.astype(BF16)
                place = slice(core * columns, (core + 1) * columns)
                out_refs[2 * i][:, place] = term[:low_rows]
                out_refs[2 * i + 1][:, place] = term[low_rows:]


def partial_terms(place, steps, grad_own, grad_other, own_weight, other_weight, after=()):
    tokens, width = grad_own.shape
    tp_count = lax.axis_size("tp")
    columns = own_weight.shape[0] // (2 * tp_count)

    def weight_spec(core):
        def index(i, s):
            step = sum(jnp.where(i == u, step, 0) for u, step in enumerate(steps))
            return ((s[1] + step) % tp_count + core * tp_count, 0)

        return pl.BlockSpec((columns, width), index)

    shape = (tokens // 2, 2 * columns)
    return pl.pallas_call(
        lambda *refs: partial_kernel(steps, *refs),
        grid_spec=pltpu.PrefetchScalarGridSpec(
            num_scalar_prefetch=1,
            grid=(len(steps),),
            in_specs=[whole((tokens, width))] * 2
            + [weight_spec(0), weight_spec(1)] * 2
            + [glance(x) for x in after],
            out_specs=[whole(shape)] * (2 * len(steps)),
        ),
        out_shape=[jax.ShapeDtypeStruct(shape, BF16)] * (2 * len(steps)),
        compiler_params=params(16),
        cost_estimate=cost(2 * len(steps)),
        name="partial_terms",
    )(place, grad_own, grad_other, own_weight, own_weight, other_weight, other_weight, *after)


def add_kernel(*refs):
    count = len(refs) // 3
    for a_ref, b_ref, out_ref in zip(refs[:count], refs[count : 2 * count], refs[2 * count :]):
        out_ref[...] = (a_ref[...].astype(jnp.float32) + b_ref[...].astype(jnp.float32)).astype(BF16)


def add_terms(held, arrived):
    return pl.pallas_call(
        add_kernel,
        grid=(1,),
        out_shape=[jax.ShapeDtypeStruct(x.shape, BF16) for x in held],
        in_specs=[whole(x.shape) for x in (*held, *arrived)],
        out_specs=[whole(x.shape) for x in held],
        compiler_params=params(16),
        cost_estimate=cost(1),
        name="add_terms",
    )(*held, *arrived)


def scatter_ring(place, across_low, across_high, *operands):
    if lax.axis_size("tp") == 2:
        own_low, own_high = partial_terms(place, (0,), *operands)
        return [own_low, shift(across_low, 1)], [own_high, shift(across_high, 1)]
    rising = shift(across_low, 1)
    falling = shift(across_high, -1)
    up_low, up_high, down_low, down_high = partial_terms(place, (1, 3), *operands)
    up_high = shift(up_high, 1)
    down_low = shift(down_low, -1)
    up_low, down_high = add_terms((up_low, down_high), (rising, falling))
    own_low, own_high = partial_terms(place, (0,), *operands, after=(up_low,))
    up_low = shift(up_low, 1)
    down_high = shift(down_high, -1)
    return [own_low, down_low, up_low], [own_high, up_high, down_high]


def sum_terms(terms):
    return sum(term[...].astype(jnp.float32) for term in terms).astype(BF16)


def give_kernel(place_ref, *refs):
    terms, out_ref = refs[:-1], refs[-1]
    count, rows = len(terms) // 2, terms[0].shape[0]
    out_ref[:rows] = sum_terms(terms[:count])
    out_ref[rows:] = sum_terms(terms[count:])


def keep_kernel(place_ref, *refs):
    terms, received_ref, out_ref = refs[:-2], refs[-2], refs[-1]
    count, rows = len(terms) // 2, terms[0].shape[0]
    side = place_ref[0]
    mine = pl.multiple_of(side * 2 * rows, 2 * rows)
    other = pl.multiple_of((1 - side) * 2 * rows, 2 * rows)
    out_ref[pl.ds(mine, rows)] = sum_terms(terms[:count])
    out_ref[pl.ds(mine + rows, rows)] = sum_terms(terms[count:])
    out_ref[pl.ds(other, 2 * rows)] = received_ref[...]


def sum_columns(place, lows, highs, received=None):
    rows, columns = lows[0].shape[0], lows[0].shape[1] // 2
    give = received is None
    extra = [] if give else [received]
    spec = pl.BlockSpec((rows, columns), lambda i, s: (0, 1 - s[0] if give else s[0]))
    out_shape = ((2 if give else 4) * rows, columns)
    return pl.pallas_call(
        give_kernel if give else keep_kernel,
        grid_spec=pltpu.PrefetchScalarGridSpec(
            num_scalar_prefetch=1,
            grid=(1,),
            in_specs=[spec] * len(lows + highs) + [whole(x.shape) for x in extra],
            out_specs=whole(out_shape),
        ),
        out_shape=jax.ShapeDtypeStruct(out_shape, BF16),
        compiler_params=params(16),
        cost_estimate=cost(1),
        name="sum_columns",
    )(place, *lows, *highs, *extra)


def shards(states, projections, neighbours, owner, slot, cotangent):
    side = lax.axis_index("grp").astype(jnp.int32)
    place = jnp.stack([side, lax.axis_index("tp").astype(jnp.int32)])
    shards_ = lax.axis_size("seq")
    tp_count = lax.axis_size("tp")
    tokens = states.shape[0] // 2
    owned, rows, features = neighbours.shape

    held = lax.dynamic_slice_in_dim(states, side * tokens, tokens, 0)
    if tp_count == 2:
        blocks, masks, last = [held], [0], [swap(held, 1)]
    else:
        low = tokens // 2
        blocks, masks = [held, swap(held, 1), swap(held, 3)], [0, 1, 3]
        last = [swap(blocks[2][:low], 1), swap(blocks[1][low:], 3)]
    own_weight = projections[0]
    other_weight = swap_cores(own_weight)
    packed = pack_rows(place, owner, slot, neighbours, shards_)
    parts = lax.all_to_all(packed, "seq", split_axis=0, concat_axis=0, tiled=True)
    routed = route_rows(parts, owned, [block[:16, :HD] for block in blocks[1:]])
    arrived = lax.all_to_all(routed, "seq", split_axis=0, concat_axis=0, tiled=True)

    sums = project(place, masks, blocks, own_weight, other_weight)
    own, other = project(place, [tp_count // 2], last, own_weight, other_weight, sums)
    near, give = unpack_rows(place, arrived, owned, rows, [own[:16, :HD]])
    far = swap_cores(give)
    grad_own, grad_other, across_low, across_high = attend(
        place, own, other, cotangent, near, far, own_weight, other_weight
    )
    lows, highs = scatter_ring(place, across_low, across_high, grad_own, grad_other, own_weight, other_weight)

    received = swap_cores(sum_columns(place, lows, highs))
    return sum_columns(place, lows, highs, received)


def solution(mesh):
    return jax.shard_map(
        shards,
        mesh=mesh,
        in_specs=(
            P("seq", "tp"),
            P("grp", None, "tp"),
            P("seq", None, "tp"),
            P("seq", None),
            P("seq", None),
            P("seq", "tp"),
        ),
        out_specs=P("seq", ("grp", "tp")),
        check_vma=False,
    )
```

```python
import jax
import jax.numpy as jnp
from jax import lax
from jax.experimental import pallas as pl
from jax.experimental.pallas import tpu as pltpu
from jax.sharding import PartitionSpec as P

HD = 128
GROUP = 64
KNB = 2
SCALE = HD ** (-0.5)
MIB = 1024 * 1024
BF16 = jnp.bfloat16


def dot_nt(a, b):
    return lax.dot_general(a, b, (((1,), (1,)), ((), ())), preferred_element_type=jnp.float32)


def dot_tn(a, b):
    return lax.dot_general(a, b, (((0,), (0,)), ((), ())), preferred_element_type=jnp.float32)


def dot_nn(a, b):
    return lax.dot_general(a, b, (((1,), (0,)), ((), ())), preferred_element_type=jnp.float32)


def params(mib=16):
    return pltpu.CompilerParams(vmem_limit_bytes=mib * MIB)


def cost(us):
    return pl.CostEstimate(flops=int(us * 1e9), bytes_accessed=int(us * 1e6), transcendentals=0)


def whole(shape):
    return pl.BlockSpec(shape, lambda *i: (0,) * len(shape))


def glance(array):
    return pl.BlockSpec((1,) * (array.ndim - 2) + (16, HD), lambda *i: (0,) * array.ndim)


def swap_cores(block):
    return lax.ppermute(block, "grp", [(0, 1), (1, 0)])


def shift(block, step):
    count = lax.axis_size("tp")
    return lax.ppermute(block, "tp", [(i, (i + step) % count) for i in range(count)])


def swap(block, mask):
    count = lax.axis_size("tp")
    return lax.ppermute(block, "tp", [(i, i ^ mask) for i in range(count)])


TABLE = 8


def batch_of(owned):
    return 8 if owned % 8 == 0 else owned


def order_matrix(batch, parts, deep, back):
    size = batch * parts * deep
    row = lax.broadcasted_iota(jnp.int32, (size, size), 0)
    column = lax.broadcasted_iota(jnp.int32, (size, size), 1)
    travel, home = (column, row) if back else (row, column)
    where = (travel % batch) * (parts * deep) + travel // batch
    return (home == where).astype(jnp.float32).astype(BF16)


def table_rows(codes, owned):
    groups = codes.shape[1]
    number = KNB * lax.broadcasted_iota(jnp.int32, (groups, HD), 0)
    column = lax.broadcasted_iota(jnp.int32, (groups, HD), 1)
    which = lax.broadcasted_iota(jnp.int32, (TABLE, HD), 0)
    table = jnp.zeros((TABLE, HD), jnp.float32)
    for i, values in enumerate((codes // 256, codes % 256)):
        values = values.astype(jnp.float32).astype(BF16)
        for k in range(KNB):
            spot = (column == number + k).astype(jnp.float32).astype(BF16)
            table = table + jnp.where(which == i, dot_nn(values, spot)[k : k + 1], 0.0)
    return table.astype(BF16)


def pack_kernel(batch, place_ref, codes_ref, neigh_ref, out_ref):
    owned, rows, half = neigh_ref.shape
    parts = out_ref.shape[0]
    deep = rows // parts
    chooser = order_matrix(batch, parts, deep, False)
    size = deep * batch
    for first in range(0, owned, batch):
        block = neigh_ref[first : first + batch].reshape(batch * rows, half)
        moved = dot_nn(chooser, block).astype(BF16).reshape(parts, size, half)
        for t in range(half // HD):
            start = (first // batch * (half // HD) + t) * size
            out_ref[:, start : start + size] = moved[:, :, t * HD : (t + 1) * HD]
    table = table_rows(codes_ref[...], owned)
    out_ref[:, owned * deep * half // HD :] = jnp.broadcast_to(table[None], (parts, TABLE, HD))


def pack_rows(place, codes, neighbours, parts):
    owned, rows, features = neighbours.shape
    half = features // 2
    message = owned * (rows // parts) * (half // HD) + TABLE
    batch = batch_of(owned)
    return pl.pallas_call(
        lambda *refs: pack_kernel(batch, *refs),
        grid_spec=pltpu.PrefetchScalarGridSpec(
            num_scalar_prefetch=1,
            grid=(1,),
            in_specs=[whole(codes.shape), pl.BlockSpec((owned, rows, half), lambda i, s: (0, 0, s[0]))],
            out_specs=whole((parts, message, HD)),
        ),
        out_shape=jax.ShapeDtypeStruct((parts, message, HD), BF16),
        compiler_params=params(16),
        cost_estimate=cost(3),
        name="pack_rows",
    )(place, codes, neighbours)


def route_kernel(owned, batch, columns, held_ref, *refs):
    out_ref = refs[-1]
    owners, message, _ = held_ref.shape
    size = (message - TABLE) * batch // (owned * columns)
    deep = size // batch
    total = owners * owned
    table = held_ref[:, message - TABLE :].astype(jnp.float32).reshape(owners * TABLE, HD).T
    held = []
    for first in range(0, owned, batch):
        pieces = []
        for t in range(columns):
            start = (first // batch * columns + t) * size
            block = held_ref[:, start : start + size].astype(jnp.float32)
            pieces += [block[:, r * batch : (r + 1) * batch].reshape(owners * batch, HD) for r in range(deep)]
        held.append(jnp.concatenate(pieces, axis=1).astype(BF16))
    held = jnp.concatenate(held, axis=0)
    lanes = lax.broadcasted_iota(jnp.int32, (owned, total), 1).astype(jnp.float32)
    per_dot = min(8, owners)
    for begin in range(0, owners, per_dot):
        choose = []
        for s in range(begin, begin + per_dot):
            high = table[:owned, s * TABLE : s * TABLE + 1]
            low = table[:owned, s * TABLE + 1 : s * TABLE + 2]
            choose.append((high * 256.0 + low == lanes).astype(jnp.float32))
        moved = dot_nn(jnp.concatenate(choose, axis=0).astype(BF16), held)
        moved = moved.reshape(per_dot, owned, columns * deep * HD)
        for first in range(0, owned, batch):
            for t in range(columns):
                start = (first // batch * columns + t) * size
                pieces = [
                    moved[:, first : first + batch, (t * deep + r) * HD : (t * deep + r + 1) * HD] for r in range(deep)
                ]
                out_ref[begin : begin + per_dot, start : start + size] = jnp.concatenate(pieces, axis=1).astype(BF16)


def route_rows(held, owned, columns, after):
    owners, message, _ = held.shape
    batch = batch_of(owned)
    out_shape = (owners, message - TABLE, HD)
    return pl.pallas_call(
        lambda *refs: route_kernel(owned, batch, columns, *refs),
        grid=(1,),
        out_shape=jax.ShapeDtypeStruct(out_shape, BF16),
        in_specs=[whole(held.shape)] + [glance(x) for x in after],
        out_specs=whole(out_shape),
        compiler_params=params(16),
        cost_estimate=cost(2),
        name="route_rows",
    )(held, *after)


def unpack_kernel(owned, batch, columns, place_ref, arrived_ref, *refs):
    keep_ref, give_ref = refs[-2:]
    parts, message, _ = arrived_ref.shape
    size = message * batch // (owned * columns)
    rows = parts * size // batch
    chooser = order_matrix(batch, parts, size // batch, True)
    mine = owned // 2
    side = place_ref[0]
    for first in range(0, owned, batch):
        starts = [(first // batch * columns + t) * size for t in range(columns)]
        block = jnp.concatenate([arrived_ref[:, x : x + size].reshape(parts * size, HD) for x in starts], axis=1)
        sorted_rows = dot_nn(chooser, block).astype(BF16)
        for n in range(first, first + batch, KNB):
            group = sorted_rows[(n - first) * rows : (n - first + KNB) * rows]
            place = pl.ds(n % mine * rows, KNB * rows)

            @pl.when(side == n // mine)
            def _():
                keep_ref[place] = group

            @pl.when(side != n // mine)
            def _():
                give_ref[place] = group


def unpack_rows(place, arrived, owned, rows, columns, after):
    batch = batch_of(owned)
    out_shape = (owned // 2 * rows, columns * HD)
    return pl.pallas_call(
        lambda *refs: unpack_kernel(owned, batch, columns, *refs),
        grid_spec=pltpu.PrefetchScalarGridSpec(
            num_scalar_prefetch=1,
            grid=(1,),
            in_specs=[whole(arrived.shape)] + [glance(x) for x in after],
            out_specs=[whole(out_shape)] * 2,
        ),
        out_shape=[jax.ShapeDtypeStruct(out_shape, BF16)] * 2,
        compiler_params=params(16),
        cost_estimate=cost(2),
        name="unpack_rows",
    )(place, arrived, *after)


def project_kernel(place_ref, *refs):
    pieces, (own_w, other_w, own_out, other_out) = refs[:-4], refs[-4:]
    step = pl.program_id(0)
    for k in range(len(pieces) // 2):

        @pl.when(step == k)
        def _():
            block = jnp.concatenate([pieces[2 * k][...], pieces[2 * k + 1][...]])
            own = dot_nn(block, own_w[...])
            other = dot_nn(block, other_w[...])
            own_out[...] = own if k == 0 else own_out[...] + own
            other_out[...] = other if k == 0 else other_out[...] + other


def project_last_kernel(place_ref, *refs):
    pieces, (own_in, other_in, own_w, other_w, own_out, other_out) = refs[:-6], refs[-6:]
    block = jnp.concatenate([piece_ref[...] for piece_ref in pieces])
    own_out[...] = (own_in[...] + dot_nn(block, own_w[...])).astype(BF16)
    other_out[...] = (other_in[...] + dot_nn(block, other_w[...])).astype(BF16)


def project(place, masks, blocks, own_weight, other_weight, sums=None):
    depth = blocks[0].shape[1]
    width = own_weight.shape[1]
    final = sums is not None
    tokens = 2 * blocks[0].shape[0]

    def mask_of(k):
        return sum(jnp.where(k == i, m, 0) for i, m in enumerate(masks))

    weight_spec = pl.BlockSpec((depth, width), lambda k, s: (s[1] ^ mask_of(k), 0))
    out_spec = whole((tokens, width))
    shape = jax.ShapeDtypeStruct((tokens, width), BF16 if final else jnp.float32)
    return pl.pallas_call(
        project_last_kernel if final else project_kernel,
        grid_spec=pltpu.PrefetchScalarGridSpec(
            num_scalar_prefetch=1,
            grid=(len(masks),),
            in_specs=[whole(x.shape) for x in blocks] + [out_spec] * (2 * final) + [weight_spec] * 2,
            out_specs=[out_spec] * 2,
        ),
        out_shape=[shape, shape],
        compiler_params=params(24),
        cost_estimate=cost(2.5 * len(masks)),
        name="project",
    )(place, *blocks, *(sums or ()), own_weight, other_weight)


def heads_gradients(items):
    queries, memory, inputs, grad_out = zip(*items)
    count = range(len(items))
    scores = [dot_nt(memory[i], inputs[i]) * SCALE for i in count]
    scores = [jnp.exp(s - jnp.max(s, axis=0, keepdims=True)) for s in scores]
    enc_probs = [s * (1.0 / jnp.sum(s, axis=0, keepdims=True)) for s in scores]
    enc_weights = [p.astype(BF16) for p in enc_probs]
    mixed = [dot_tn(enc_weights[i], memory[i]) for i in count]
    keys = [(inputs[i].astype(jnp.float32) + mixed[i]).astype(BF16) for i in count]
    scores = [dot_nt(queries[i], keys[i]) * SCALE for i in count]
    grad_probs = [dot_nt(grad_out[i], keys[i]) for i in count]
    scores = [jnp.exp(s - jnp.max(s, axis=1, keepdims=True)) for s in scores]
    probs = [s * (1.0 / jnp.sum(s, axis=1, keepdims=True)) for s in scores]
    weights = [p.astype(BF16) for p in probs]
    from_values = [dot_tn(weights[i], grad_out[i]) for i in count]
    grad_scores = [p * (g - jnp.sum(p * g, axis=1, keepdims=True)) for p, g in zip(probs, grad_probs)]
    grad_scores = [g.astype(BF16) for g in grad_scores]
    grad_keys = [dot_tn(grad_scores[i], queries[i]) * SCALE + from_values[i] for i in count]
    grad_keys = [g.astype(BF16) for g in grad_keys]
    grad_queries = [(dot_nn(grad_scores[i], keys[i]) * SCALE).astype(BF16) for i in count]
    grad_probs = [dot_nt(memory[i], grad_keys[i]) for i in count]
    from_values = [dot_nn(enc_weights[i], grad_keys[i]) for i in count]
    grad_scores = [p * (g - jnp.sum(p * g, axis=0, keepdims=True)) for p, g in zip(enc_probs, grad_probs)]
    grad_scores = [g.astype(BF16) for g in grad_scores]
    grad_memory = [(dot_nn(grad_scores[i], inputs[i]) * SCALE + from_values[i]).astype(BF16) for i in count]
    return grad_queries, grad_memory


def attend_kernel(
    tp_count, far_step, place_ref, own_ref, other_ref, cot_ref, near_ref, far_ref, own_hbm, other_hbm,
    grad_own_ref, grad_other_ref, low_ref, high_ref, weights, arrived,
):
    step = pl.program_id(0)
    side = place_ref[0]
    columns = weights.shape[1]
    target = (place_ref[1] + far_step) % tp_count
    copies = [
        pltpu.make_async_copy(
            hbm.at[pl.ds(pl.multiple_of((target + core * tp_count) * columns, columns), columns)],
            weights.at[2 * core + i],
            arrived.at[2 * core + i],
        )
        for core in range(2)
        for i, hbm in enumerate((own_hbm, other_hbm))
    ]

    @pl.when(step == 0)
    def _():
        for copy in copies:
            copy.start()

    half = near_ref.shape[1]
    first = side == 0
    tokens = own_ref.shape[0]
    groups = tokens // GROUP
    keys = near_ref.shape[0] // groups
    items, spots = [], []
    for c in range(groups):
        rows = slice(c * GROUP, (c + 1) * GROUP)
        place = pl.ds(pl.multiple_of(step * tokens + c * GROUP, GROUP), GROUP)
        for far, held_ref in enumerate((near_ref, far_ref)):
            start = ((side + far) % 2) * half
            for low in range(0, half, HD):
                lanes = pl.ds(pl.multiple_of(start + low, HD), HD)
                own = own_ref[rows, lanes]
                other = other_ref[rows, lanes]
                items.append(
                    (
                        jnp.where(first, own, other),
                        jnp.where(first, other, own),
                        held_ref[c * keys : (c + 1) * keys, low : low + HD],
                        cot_ref[rows, lanes],
                    )
                )
                spots.append((place, lanes))
    grad_queries, grad_memory = heads_gradients(items)
    for spot, grad_q, grad_m in zip(spots, grad_queries, grad_memory):
        grad_own_ref[spot] = jnp.where(first, grad_q, grad_m)
        grad_other_ref[spot] = jnp.where(first, grad_m, grad_q)

    @pl.when(step == pl.num_programs(0) - 1)
    def _():
        for copy in copies:
            copy.wait()
        low_rows = low_ref.shape[0]
        grad_own, grad_other = grad_own_ref[...], grad_other_ref[...]
        for core in range(2):
            term = dot_nt(grad_own, weights[2 * core]) + dot_nt(grad_other, weights[2 * core + 1])
            term = term.astype(BF16)
            low_ref[:, core * columns : (core + 1) * columns] = term[:low_rows]
            high_ref[:, core * columns : (core + 1) * columns] = term[low_rows:]


def attend(place, own, other, cotangent, near, far, own_weight, other_weight):
    tokens, width = own.shape
    rows, half = near.shape
    groups = tokens // GROUP
    steps = groups // 3 if groups % 3 == 0 else groups
    tp_count = lax.axis_size("tp")
    columns = own_weight.shape[0] // (2 * tp_count)
    token_spec = pl.BlockSpec((tokens // steps, width), lambda c, s: (c, 0))
    cot_spec = pl.BlockSpec((tokens // steps, width), lambda c, s: (s[0] * steps + c, 0))
    neigh_spec = pl.BlockSpec((rows // steps, half), lambda c, s: (c, 0))
    outs = [(tokens, width)] * 2 + [(tokens // 2, 2 * columns)] * 2
    return pl.pallas_call(
        lambda *refs: attend_kernel(tp_count, tp_count // 2, *refs),
        grid_spec=pltpu.PrefetchScalarGridSpec(
            num_scalar_prefetch=1,
            grid=(steps,),
            in_specs=[token_spec] * 2 + [cot_spec] + [neigh_spec] * 2 + [pl.BlockSpec(memory_space=pl.ANY)] * 2,
            out_specs=[whole(shape) for shape in outs],
            scratch_shapes=[pltpu.VMEM((4, columns, width), BF16), pltpu.SemaphoreType.DMA((4,))],
        ),
        out_shape=[jax.ShapeDtypeStruct(shape, BF16) for shape in outs],
        compiler_params=params(16),
        cost_estimate=cost(8),
        name="attend",
    )(place, own, other, cotangent, near, far, own_weight, other_weight)


def partial_kernel(steps, place_ref, own_ref, other_ref, own_a, own_b, other_a, other_b, *refs):
    out_refs = refs[-2 * len(steps) :]
    columns = own_a.shape[0]
    low_rows = own_ref.shape[0] // 2
    for i in range(len(steps)):

        @pl.when(pl.program_id(0) == i)
        def _():
            own, other = own_ref[...], other_ref[...]
            for core, weights in enumerate(((own_a, other_a), (own_b, other_b))):
                term = dot_nt(own, weights[0][...]) + dot_nt(other, weights[1][...])
                term = term.astype(BF16)
                place = slice(core * columns, (core + 1) * columns)
                out_refs[2 * i][:, place] = term[:low_rows]
                out_refs[2 * i + 1][:, place] = term[low_rows:]


def partial_terms(place, steps, grad_own, grad_other, own_weight, other_weight, after=()):
    tokens, width = grad_own.shape
    tp_count = lax.axis_size("tp")
    columns = own_weight.shape[0] // (2 * tp_count)

    def weight_spec(core):
        def index(i, s):
            step = sum(jnp.where(i == u, step, 0) for u, step in enumerate(steps))
            return ((s[1] + step) % tp_count + core * tp_count, 0)

        return pl.BlockSpec((columns, width), index)

    shape = (tokens // 2, 2 * columns)
    return pl.pallas_call(
        lambda *refs: partial_kernel(steps, *refs),
        grid_spec=pltpu.PrefetchScalarGridSpec(
            num_scalar_prefetch=1,
            grid=(len(steps),),
            in_specs=[whole((tokens, width))] * 2
            + [weight_spec(0), weight_spec(1)] * 2
            + [glance(x) for x in after],
            out_specs=[whole(shape)] * (2 * len(steps)),
        ),
        out_shape=[jax.ShapeDtypeStruct(shape, BF16)] * (2 * len(steps)),
        compiler_params=params(16),
        cost_estimate=cost(2 * len(steps)),
        name="partial_terms",
    )(place, grad_own, grad_other, own_weight, own_weight, other_weight, other_weight, *after)


def add_kernel(*refs):
    count = len(refs) // 3
    for a_ref, b_ref, out_ref in zip(refs[:count], refs[count : 2 * count], refs[2 * count :]):
        out_ref[...] = (a_ref[...].astype(jnp.float32) + b_ref[...].astype(jnp.float32)).astype(BF16)


def add_terms(held, arrived):
    return pl.pallas_call(
        add_kernel,
        grid=(1,),
        out_shape=[jax.ShapeDtypeStruct(x.shape, BF16) for x in held],
        in_specs=[whole(x.shape) for x in (*held, *arrived)],
        out_specs=[whole(x.shape) for x in held],
        compiler_params=params(16),
        cost_estimate=cost(1),
        name="add_terms",
    )(*held, *arrived)


def scatter_ring(place, across_low, across_high, *operands):
    if lax.axis_size("tp") == 2:
        own_low, own_high = partial_terms(place, (0,), *operands)
        return [own_low, shift(across_low, 1)], [own_high, shift(across_high, 1)]
    rising = shift(across_low, 1)
    falling = shift(across_high, -1)
    up_low, up_high, down_low, down_high = partial_terms(place, (1, 3), *operands)
    up_high = shift(up_high, 1)
    down_low = shift(down_low, -1)
    up_low, down_high = add_terms((up_low, down_high), (rising, falling))
    own_low, own_high = partial_terms(place, (0,), *operands, after=(up_low,))
    up_low = shift(up_low, 1)
    down_high = shift(down_high, -1)
    return [own_low, down_low, up_low], [own_high, up_high, down_high]


def sum_terms(terms):
    return sum(term[...].astype(jnp.float32) for term in terms).astype(BF16)


def give_kernel(place_ref, *refs):
    terms, out_ref = refs[:-1], refs[-1]
    count, rows = len(terms) // 2, terms[0].shape[0]
    out_ref[:rows] = sum_terms(terms[:count])
    out_ref[rows:] = sum_terms(terms[count:])


def keep_kernel(place_ref, *refs):
    terms, received_ref, out_ref = refs[:-2], refs[-2], refs[-1]
    count, rows = len(terms) // 2, terms[0].shape[0]
    side = place_ref[0]
    mine = pl.multiple_of(side * 2 * rows, 2 * rows)
    other = pl.multiple_of((1 - side) * 2 * rows, 2 * rows)
    out_ref[pl.ds(mine, rows)] = sum_terms(terms[:count])
    out_ref[pl.ds(mine + rows, rows)] = sum_terms(terms[count:])
    out_ref[pl.ds(other, 2 * rows)] = received_ref[...]


def sum_columns(place, lows, highs, received=None):
    rows, columns = lows[0].shape[0], lows[0].shape[1] // 2
    give = received is None
    extra = [] if give else [received]
    spec = pl.BlockSpec((rows, columns), lambda i, s: (0, 1 - s[0] if give else s[0]))
    out_shape = ((2 if give else 4) * rows, columns)
    return pl.pallas_call(
        give_kernel if give else keep_kernel,
        grid_spec=pltpu.PrefetchScalarGridSpec(
            num_scalar_prefetch=1,
            grid=(1,),
            in_specs=[spec] * len(lows + highs) + [whole(x.shape) for x in extra],
            out_specs=whole(out_shape),
        ),
        out_shape=jax.ShapeDtypeStruct(out_shape, BF16),
        compiler_params=params(16),
        cost_estimate=cost(1),
        name="sum_columns",
    )(place, *lows, *highs, *extra)


def shards(states, projections, neighbours, owner, slot, cotangent):
    side = lax.axis_index("grp").astype(jnp.int32)
    place = jnp.stack([side, lax.axis_index("tp").astype(jnp.int32)])
    shards_ = lax.axis_size("seq")
    tp_count = lax.axis_size("tp")
    tokens = states.shape[0] // 2
    owned, rows, features = neighbours.shape

    low = tokens // 2
    held = [lax.dynamic_slice_in_dim(states, side * tokens + first, low, 0) for first in (0, low)]
    if tp_count == 2:
        blocks, masks, early, last = held, [0], [], [swap(x, 1) for x in held]
    else:
        masks = [0, 1, 3]
        near1, near3 = ([swap(x, mask) for x in held] for mask in masks[1:])
        blocks = held + near1 + near3
        last = [swap(near3[0], 1), swap(near1[1], 3)]
        early = near1 + near3
    own_weight = projections[0]
    other_weight = swap_cores(own_weight)

    batch = batch_of(owned)
    columns = features // 2 // HD
    owner, slot = owner.T, slot.T
    codes = slot // batch * (shards_ * batch) + owner * batch + slot % batch
    packed = pack_rows(place, codes, neighbours, shards_)
    parts = lax.all_to_all(packed, "seq", split_axis=0, concat_axis=0, tiled=True)
    routed = route_rows(parts, owned, columns, [x[:16, :HD] for x in early])
    arrived = lax.all_to_all(routed, "seq", split_axis=0, concat_axis=0, tiled=True)

    sums = project(place, masks, blocks, own_weight, other_weight)
    own, other = project(place, [tp_count // 2], last, own_weight, other_weight, sums)
    near, give = unpack_rows(place, arrived, owned, rows, columns, [own[:16, :HD]])
    far = swap_cores(give)
    grad_own, grad_other, across_low, across_high = attend(
        place, own, other, cotangent, near, far, own_weight, other_weight
    )
    lows, highs = scatter_ring(place, across_low, across_high, grad_own, grad_other, own_weight, other_weight)

    received = swap_cores(sum_columns(place, lows, highs))
    return sum_columns(place, lows, highs, received)


def solution(mesh):
    return jax.shard_map(
        shards,
        mesh=mesh,
        in_specs=(
            P("seq", "tp"),
            P("grp", None, "tp"),
            P("seq", None, "tp"),
            P("seq", None),
            P("seq", None),
            P("seq", "tp"),
        ),
        out_specs=P("seq", ("grp", "tp")),
        check_vma=False,
    )
```

```python
import jax
import jax.numpy as jnp
from jax import lax
from jax.experimental import pallas as pl
from jax.experimental.pallas import tpu as pltpu
from jax.sharding import PartitionSpec as P

HD = 128
GROUP = 64
KNB = 2
SCALE = HD ** (-0.5)
MIB = 1024 * 1024
BF16 = jnp.bfloat16


def dot_nt(a, b):
    return lax.dot_general(a, b, (((1,), (1,)), ((), ())), preferred_element_type=jnp.float32)


def dot_tn(a, b):
    return lax.dot_general(a, b, (((0,), (0,)), ((), ())), preferred_element_type=jnp.float32)


def dot_nn(a, b):
    return lax.dot_general(a, b, (((1,), (0,)), ((), ())), preferred_element_type=jnp.float32)


def params(mib=16):
    return pltpu.CompilerParams(vmem_limit_bytes=mib * MIB)


def cost(us):
    return pl.CostEstimate(flops=int(us * 1e9), bytes_accessed=int(us * 1e6), transcendentals=0)


def whole(shape):
    return pl.BlockSpec(shape, lambda *i: (0,) * len(shape))


def glance(array):
    return pl.BlockSpec((1,) * (array.ndim - 2) + (16, HD), lambda *i: (0,) * array.ndim)


def swap_cores(block):
    return lax.ppermute(block, "grp", [(0, 1), (1, 0)])


def swap(block, mask):
    count = lax.axis_size("tp")
    return lax.ppermute(block, "tp", [(i, i ^ mask) for i in range(count)])


TABLE = 8


def batch_of(owned):
    return 8 if owned % 8 == 0 else owned


def order_matrix(batch, parts, deep, back):
    size = batch * parts * deep
    row = lax.broadcasted_iota(jnp.int32, (size, size), 0)
    column = lax.broadcasted_iota(jnp.int32, (size, size), 1)
    travel, home = (column, row) if back else (row, column)
    where = (travel % batch) * (parts * deep) + travel // batch
    return (home == where).astype(jnp.float32).astype(BF16)


def table_rows(codes, owned):
    groups = codes.shape[1]
    group = lax.broadcasted_iota(jnp.int32, (groups, HD), 0)
    count = batch_of(owned) // (2 * KNB)
    core, group = group // (groups // 2), group % (groups // 2)
    number = KNB * (group // count * (2 * count) + core * count + group % count)
    column = lax.broadcasted_iota(jnp.int32, (groups, HD), 1)
    which = lax.broadcasted_iota(jnp.int32, (TABLE, HD), 0)
    table = jnp.zeros((TABLE, HD), jnp.float32)
    for i, values in enumerate((codes // 256, codes % 256)):
        values = values.astype(jnp.float32).astype(BF16)
        for k in range(KNB):
            spot = (column == number + k).astype(jnp.float32).astype(BF16)
            table = table + jnp.where(which == i, dot_nn(values, spot)[k : k + 1], 0.0)
    return table.astype(BF16)


def pack_kernel(batch, place_ref, codes_ref, neigh_ref, out_ref):
    owned, rows, half = neigh_ref.shape
    parts = out_ref.shape[0]
    deep = rows // parts
    chooser = order_matrix(batch, parts, deep, False)
    size = deep * batch
    for first in range(0, owned, batch):
        block = neigh_ref[first : first + batch].reshape(batch * rows, half)
        moved = dot_nn(chooser, block).astype(BF16).reshape(parts, size, half)
        for t in range(half // HD):
            start = (first // batch * (half // HD) + t) * size
            out_ref[:, start : start + size] = moved[:, :, t * HD : (t + 1) * HD]
    table = table_rows(codes_ref[...], owned)
    out_ref[:, owned * deep * half // HD :] = jnp.broadcast_to(table[None], (parts, TABLE, HD))


def pack_rows(place, codes, neighbours, parts):
    owned, rows, features = neighbours.shape
    half = features // 2
    message = owned * (rows // parts) * (half // HD) + TABLE
    batch = batch_of(owned)
    return pl.pallas_call(
        lambda *refs: pack_kernel(batch, *refs),
        grid_spec=pltpu.PrefetchScalarGridSpec(
            num_scalar_prefetch=1,
            grid=(1,),
            in_specs=[whole(codes.shape), pl.BlockSpec((owned, rows, half), lambda i, s: (0, 0, s[0]))],
            out_specs=whole((parts, message, HD)),
        ),
        out_shape=jax.ShapeDtypeStruct((parts, message, HD), BF16),
        compiler_params=params(16),
        cost_estimate=cost(3),
        name="pack_rows",
    )(place, codes, neighbours)


def route_kernel(owned, batch, columns, held_ref, *refs):
    out_ref = refs[-1]
    owners, message, _ = held_ref.shape
    size = (message - TABLE) * batch // (owned * columns)
    deep = size // batch
    total = owners * owned
    table = held_ref[:, message - TABLE :].astype(jnp.float32).reshape(owners * TABLE, HD).T
    held = []
    for first in range(0, owned, batch):
        pieces = []
        for t in range(columns):
            start = (first // batch * columns + t) * size
            block = held_ref[:, start : start + size].astype(jnp.float32)
            pieces += [block[:, r * batch : (r + 1) * batch].reshape(owners * batch, HD) for r in range(deep)]
        held.append(jnp.concatenate(pieces, axis=1).astype(BF16))
    held = jnp.concatenate(held, axis=0)
    lanes = lax.broadcasted_iota(jnp.int32, (owned, total), 1).astype(jnp.float32)
    per_dot = min(16, owners)
    for begin in range(0, owners, per_dot):
        choose = []
        for s in range(begin, begin + per_dot):
            high = table[:owned, s * TABLE : s * TABLE + 1]
            low = table[:owned, s * TABLE + 1 : s * TABLE + 2]
            choose.append((high * 256.0 + low == lanes).astype(jnp.float32))
        moved = dot_nn(jnp.concatenate(choose, axis=0).astype(BF16), held)
        moved = moved.reshape(per_dot, owned, columns * deep * HD)
        for first in range(0, owned, batch):
            for t in range(columns):
                start = (first // batch * columns + t) * size
                pieces = [
                    moved[:, first : first + batch, (t * deep + r) * HD : (t * deep + r + 1) * HD] for r in range(deep)
                ]
                out_ref[begin : begin + per_dot, start : start + size] = jnp.concatenate(pieces, axis=1).astype(BF16)


def route_rows(held, owned, columns, after):
    owners, message, _ = held.shape
    batch = batch_of(owned)
    out_shape = (owners, message - TABLE, HD)
    return pl.pallas_call(
        lambda *refs: route_kernel(owned, batch, columns, *refs),
        grid=(1,),
        out_shape=jax.ShapeDtypeStruct(out_shape, BF16),
        in_specs=[whole(held.shape)] + [glance(x) for x in after],
        out_specs=whole(out_shape),
        compiler_params=params(16),
        cost_estimate=cost(2),
        name="route_rows",
    )(held, *after)


def unpack_kernel(owned, batch, columns, partner, place_ref, arrived_ref, *refs):
    out_ref = refs[-1]
    parts, message, _ = arrived_ref.shape
    size = message * batch // (owned * columns)
    rows = parts * size // batch
    chooser = order_matrix(batch, parts, size // batch, True)
    count = batch // 2
    side = place_ref[0] ^ partner
    for first in range(0, owned, batch):
        starts = [(first // batch * columns + t) * size for t in range(columns)]
        block = jnp.concatenate([arrived_ref[:, x : x + size].reshape(parts * size, HD) for x in starts], axis=1)
        chosen = jnp.where(side == 0, chooser[: count * rows], chooser[count * rows :])
        out_ref[first // 2 * rows : (first // 2 + count) * rows] = dot_nn(chosen, block).astype(BF16)


def unpack_rows(place, arrived, owned, rows, columns, partner, after):
    batch = batch_of(owned)
    out_shape = (owned // 2 * rows, columns * HD)
    return pl.pallas_call(
        lambda *refs: unpack_kernel(owned, batch, columns, partner, *refs),
        grid_spec=pltpu.PrefetchScalarGridSpec(
            num_scalar_prefetch=1,
            grid=(1,),
            in_specs=[whole(arrived.shape)] + [glance(x) for x in after],
            out_specs=whole(out_shape),
        ),
        out_shape=jax.ShapeDtypeStruct(out_shape, BF16),
        compiler_params=params(16),
        cost_estimate=cost(1),
        name="unpack_rows",
    )(place, arrived, *after)


def project_kernel(place_ref, *refs):
    pieces, (own_w, other_w, own_out, other_out) = refs[:-4], refs[-4:]
    step = pl.program_id(0)
    for k in range(len(pieces) // 2):

        @pl.when(step == k)
        def _():
            block = jnp.concatenate([pieces[2 * k][...], pieces[2 * k + 1][...]])
            own = dot_nn(block, own_w[...])
            other = dot_nn(block, other_w[...])
            own_out[...] = own if k == 0 else own_out[...] + own
            other_out[...] = other if k == 0 else other_out[...] + other


def project_last_kernel(place_ref, *refs):
    pieces, (own_in, other_in, own_w, other_w, own_out, other_out) = refs[:-6], refs[-6:]
    block = jnp.concatenate([piece_ref[...] for piece_ref in pieces])
    own_out[...] = (own_in[...] + dot_nn(block, own_w[...])).astype(BF16)
    other_out[...] = (other_in[...] + dot_nn(block, other_w[...])).astype(BF16)


def project(place, masks, blocks, own_weight, other_weight, sums=None):
    depth = blocks[0].shape[1]
    width = own_weight.shape[1]
    final = sums is not None
    tokens = 2 * blocks[0].shape[0]

    def mask_of(k):
        return sum(jnp.where(k == i, m, 0) for i, m in enumerate(masks))

    weight_spec = pl.BlockSpec((depth, width), lambda k, s: (s[1] ^ mask_of(k), 0))
    out_spec = whole((tokens, width))
    shape = jax.ShapeDtypeStruct((tokens, width), BF16 if final else jnp.float32)
    return pl.pallas_call(
        project_last_kernel if final else project_kernel,
        grid_spec=pltpu.PrefetchScalarGridSpec(
            num_scalar_prefetch=1,
            grid=(len(masks),),
            in_specs=[whole(x.shape) for x in blocks] + [out_spec] * (2 * final) + [weight_spec] * 2,
            out_specs=[out_spec] * 2,
        ),
        out_shape=[shape, shape],
        compiler_params=params(24),
        cost_estimate=cost(2.5 * len(masks)),
        name="project",
    )(place, *blocks, *(sums or ()), own_weight, other_weight)


def heads_gradients(items):
    queries, memory, inputs, grad_out = zip(*items)
    count = range(len(items))
    scores = [dot_nt(memory[i], inputs[i]) * SCALE for i in count]
    scores = [jnp.exp(s - jnp.max(s, axis=0, keepdims=True)) for s in scores]
    enc_probs = [s * (1.0 / jnp.sum(s, axis=0, keepdims=True)) for s in scores]
    enc_weights = [p.astype(BF16) for p in enc_probs]
    mixed = [dot_tn(enc_weights[i], memory[i]) for i in count]
    keys = [(inputs[i].astype(jnp.float32) + mixed[i]).astype(BF16) for i in count]
    scores = [dot_nt(queries[i], keys[i]) * SCALE for i in count]
    grad_probs = [dot_nt(grad_out[i], keys[i]) for i in count]
    scores = [jnp.exp(s - jnp.max(s, axis=1, keepdims=True)) for s in scores]
    probs = [s * (1.0 / jnp.sum(s, axis=1, keepdims=True)) for s in scores]
    weights = [p.astype(BF16) for p in probs]
    from_values = [dot_tn(weights[i], grad_out[i]) for i in count]
    grad_scores = [p * (g - jnp.sum(p * g, axis=1, keepdims=True)) for p, g in zip(probs, grad_probs)]
    grad_scores = [g.astype(BF16) for g in grad_scores]
    grad_keys = [dot_tn(grad_scores[i], queries[i]) * SCALE + from_values[i] for i in count]
    grad_keys = [g.astype(BF16) for g in grad_keys]
    grad_queries = [(dot_nn(grad_scores[i], keys[i]) * SCALE).astype(BF16) for i in count]
    grad_probs = [dot_nt(memory[i], grad_keys[i]) for i in count]
    from_values = [dot_nn(enc_weights[i], grad_keys[i]) for i in count]
    grad_scores = [p * (g - jnp.sum(p * g, axis=0, keepdims=True)) for p, g in zip(enc_probs, grad_probs)]
    grad_scores = [g.astype(BF16) for g in grad_scores]
    grad_memory = [(dot_nn(grad_scores[i], inputs[i]) * SCALE + from_values[i]).astype(BF16) for i in count]
    return grad_queries, grad_memory


def attend_kernel(
    tp_count, place_ref, own_ref, other_ref, cot_ref, near_ref, far_ref, own_hbm, other_hbm,
    grad_own_ref, grad_other_ref, low_ref, high_ref, weights, arrived,
):
    step = pl.program_id(0)
    side = place_ref[0]
    columns = weights.shape[1]
    target = place_ref[1] ^ (tp_count // 2)
    copies = [
        pltpu.make_async_copy(
            hbm.at[pl.ds(pl.multiple_of((target + core * tp_count) * columns, columns), columns)],
            weights.at[2 * core + i],
            arrived.at[2 * core + i],
        )
        for core in range(2)
        for i, hbm in enumerate((own_hbm, other_hbm))
    ]

    @pl.when(step == 0)
    def _():
        for copy in copies:
            copy.start()

    half = near_ref.shape[1]
    first = side == 0
    tokens = own_ref.shape[0]
    groups = tokens // GROUP
    keys = near_ref.shape[0] // groups
    items, spots = [], []
    for c in range(groups):
        rows = slice(c * GROUP, (c + 1) * GROUP)
        place = pl.ds(pl.multiple_of(step * tokens + c * GROUP, GROUP), GROUP)
        for far, held_ref in enumerate((near_ref, far_ref)):
            start = ((side + far) % 2) * half
            for low in range(0, half, HD):
                lanes = pl.ds(pl.multiple_of(start + low, HD), HD)
                own = own_ref[rows, lanes]
                other = other_ref[rows, lanes]
                items.append(
                    (
                        jnp.where(first, own, other),
                        jnp.where(first, other, own),
                        held_ref[c * keys : (c + 1) * keys, low : low + HD],
                        cot_ref[rows, lanes],
                    )
                )
                spots.append((place, lanes))
    grad_queries, grad_memory = heads_gradients(items)
    for spot, grad_q, grad_m in zip(spots, grad_queries, grad_memory):
        grad_own_ref[spot] = jnp.where(first, grad_q, grad_m)
        grad_other_ref[spot] = jnp.where(first, grad_m, grad_q)

    @pl.when(step == pl.num_programs(0) - 1)
    def _():
        for copy in copies:
            copy.wait()
        low_rows = low_ref.shape[0]
        grad_own, grad_other = grad_own_ref[...], grad_other_ref[...]
        for core in range(2):
            term = dot_nt(grad_own, weights[2 * core]) + dot_nt(grad_other, weights[2 * core + 1])
            term = term.astype(BF16)
            low_ref[:, core * columns : (core + 1) * columns] = term[:low_rows]
            high_ref[:, core * columns : (core + 1) * columns] = term[low_rows:]


def attend(place, own, other, cotangent, near, far, own_weight, other_weight):
    tokens, width = own.shape
    rows, half = near.shape
    groups = tokens // GROUP
    steps = groups // 3 if groups % 3 == 0 else groups
    tp_count = lax.axis_size("tp")
    columns = own_weight.shape[0] // (2 * tp_count)
    token_spec = pl.BlockSpec((tokens // steps, width), lambda c, s: (c, 0))
    cot_spec = pl.BlockSpec((tokens // steps, width), lambda c, s: (s[0] * steps + c, 0))
    neigh_spec = pl.BlockSpec((rows // steps, half), lambda c, s: (c, 0))
    outs = [(tokens, width)] * 2 + [(tokens // 2, 2 * columns)] * 2
    return pl.pallas_call(
        lambda *refs: attend_kernel(tp_count, *refs),
        grid_spec=pltpu.PrefetchScalarGridSpec(
            num_scalar_prefetch=1,
            grid=(steps,),
            in_specs=[token_spec] * 2 + [cot_spec] + [neigh_spec] * 2 + [pl.BlockSpec(memory_space=pl.ANY)] * 2,
            out_specs=[whole(shape) for shape in outs],
            scratch_shapes=[pltpu.VMEM((4, columns, width), BF16), pltpu.SemaphoreType.DMA((4,))],
        ),
        out_shape=[jax.ShapeDtypeStruct(shape, BF16) for shape in outs],
        compiler_params=params(16),
        cost_estimate=cost(8),
        name="attend",
    )(place, own, other, cotangent, near, far, own_weight, other_weight)


def partial_kernel(masks, place_ref, own_ref, other_ref, own_a, own_b, other_a, other_b, *refs):
    out_refs = refs[-2 * len(masks) :]
    columns = own_a.shape[0]
    low_rows = own_ref.shape[0] // 2
    for i in range(len(masks)):

        @pl.when(pl.program_id(0) == i)
        def _():
            own, other = own_ref[...], other_ref[...]
            for core, weights in enumerate(((own_a, other_a), (own_b, other_b))):
                term = dot_nt(own, weights[0][...]) + dot_nt(other, weights[1][...])
                term = term.astype(BF16)
                place = slice(core * columns, (core + 1) * columns)
                out_refs[2 * i][:, place] = term[:low_rows]
                out_refs[2 * i + 1][:, place] = term[low_rows:]


def partial_terms(place, masks, grad_own, grad_other, own_weight, other_weight, after=()):
    tokens, width = grad_own.shape
    tp_count = lax.axis_size("tp")
    columns = own_weight.shape[0] // (2 * tp_count)

    def weight_spec(core):
        def index(i, s):
            mask = sum(jnp.where(i == u, mask, 0) for u, mask in enumerate(masks))
            return ((s[1] ^ mask) + core * tp_count, 0)

        return pl.BlockSpec((columns, width), index)

    shape = (tokens // 2, 2 * columns)
    return pl.pallas_call(
        lambda *refs: partial_kernel(masks, *refs),
        grid_spec=pltpu.PrefetchScalarGridSpec(
            num_scalar_prefetch=1,
            grid=(len(masks),),
            in_specs=[whole((tokens, width))] * 2
            + [weight_spec(0), weight_spec(1)] * 2
            + [glance(x) for x in after],
            out_specs=[whole(shape)] * (2 * len(masks)),
        ),
        out_shape=[jax.ShapeDtypeStruct(shape, BF16)] * (2 * len(masks)),
        compiler_params=params(16),
        cost_estimate=cost(2 * len(masks)),
        name="partial_terms",
    )(place, grad_own, grad_other, own_weight, own_weight, other_weight, other_weight, *after)


def add_kernel(*refs):
    count = len(refs) // 3
    for a_ref, b_ref, out_ref in zip(refs[:count], refs[count : 2 * count], refs[2 * count :]):
        out_ref[...] = (a_ref[...].astype(jnp.float32) + b_ref[...].astype(jnp.float32)).astype(BF16)


def add_terms(held, arrived):
    return pl.pallas_call(
        add_kernel,
        grid=(1,),
        out_shape=[jax.ShapeDtypeStruct(x.shape, BF16) for x in held],
        in_specs=[whole(x.shape) for x in (*held, *arrived)],
        out_specs=[whole(x.shape) for x in held],
        compiler_params=params(16),
        cost_estimate=cost(1),
        name="add_terms",
    )(*held, *arrived)


def scatter_ring(place, across_low, across_high, *operands):
    if lax.axis_size("tp") == 2:
        own_low, own_high = partial_terms(place, (0,), *operands)
        return [own_low, swap(across_low, 1)], [own_high, swap(across_high, 1)]
    from1 = swap(across_low, 1)
    from3 = swap(across_high, 3)
    low3, high3, low1, high1 = partial_terms(place, (3, 1), *operands)
    high3 = swap(high3, 3)
    low1 = swap(low1, 1)
    low3, high1 = add_terms((low3, high1), (from1, from3))
    own_low, own_high = partial_terms(place, (0,), *operands, after=(low3,))
    low3 = swap(low3, 3)
    high1 = swap(high1, 1)
    return [own_low, low1, low3], [own_high, high3, high1]


def sum_terms(terms):
    return sum(term[...].astype(jnp.float32) for term in terms).astype(BF16)


def give_kernel(place_ref, *refs):
    terms, out_ref = refs[:-1], refs[-1]
    count, rows = len(terms) // 2, terms[0].shape[0]
    out_ref[:rows] = sum_terms(terms[:count])
    out_ref[rows:] = sum_terms(terms[count:])


def keep_kernel(place_ref, *refs):
    terms, received_ref, out_ref = refs[:-2], refs[-2], refs[-1]
    count, rows = len(terms) // 2, terms[0].shape[0]
    side = place_ref[0]
    mine = pl.multiple_of(side * 2 * rows, 2 * rows)
    other = pl.multiple_of((1 - side) * 2 * rows, 2 * rows)
    out_ref[pl.ds(mine, rows)] = sum_terms(terms[:count])
    out_ref[pl.ds(mine + rows, rows)] = sum_terms(terms[count:])
    out_ref[pl.ds(other, 2 * rows)] = received_ref[...]


def sum_columns(place, lows, highs, received=None):
    rows, columns = lows[0].shape[0], lows[0].shape[1] // 2
    give = received is None
    extra = [] if give else [received]
    spec = pl.BlockSpec((rows, columns), lambda i, s: (0, 1 - s[0] if give else s[0]))
    out_shape = ((2 if give else 4) * rows, columns)
    return pl.pallas_call(
        give_kernel if give else keep_kernel,
        grid_spec=pltpu.PrefetchScalarGridSpec(
            num_scalar_prefetch=1,
            grid=(1,),
            in_specs=[spec] * len(lows + highs) + [whole(x.shape) for x in extra],
            out_specs=whole(out_shape),
        ),
        out_shape=jax.ShapeDtypeStruct(out_shape, BF16),
        compiler_params=params(16),
        cost_estimate=cost(1),
        name="sum_columns",
    )(place, *lows, *highs, *extra)


def shards(states, projections, neighbours, owner, slot, cotangent):
    side = lax.axis_index("grp").astype(jnp.int32)
    place = jnp.stack([side, lax.axis_index("tp").astype(jnp.int32)])
    shards_ = lax.axis_size("seq")
    tp_count = lax.axis_size("tp")
    tokens = states.shape[0] // 2
    owned, rows, features = neighbours.shape

    low = tokens // 2
    held = [lax.dynamic_slice_in_dim(states, side * tokens + first, low, 0) for first in (0, low)]
    if tp_count == 2:
        blocks, masks, early, last = held, [0], [], [swap(x, 1) for x in held]
    else:
        masks = [0, 1, 3]
        near1, near3 = ([swap(x, mask) for x in held] for mask in masks[1:])
        blocks = held + near1 + near3
        last = [swap(near3[0], 1), swap(near1[1], 3)]
        early = near1 + near3
    own_weight = projections[0]
    other_weight = swap_cores(own_weight)

    batch = batch_of(owned)
    columns = features // 2 // HD
    owner, slot = owner.T, slot.T
    codes = slot // batch * (shards_ * batch) + owner * batch + slot % batch
    packed = pack_rows(place, codes, neighbours, shards_)
    parts = lax.all_to_all(packed, "seq", split_axis=0, concat_axis=0, tiled=True)
    routed = route_rows(parts, owned, columns, [x[:16, :HD] for x in early])
    arrived = lax.all_to_all(routed, "seq", split_axis=0, concat_axis=0, tiled=True)

    sums = project(place, masks, blocks, own_weight, other_weight)
    own, other = project(place, [tp_count // 2], last, own_weight, other_weight, sums)
    give = unpack_rows(place, arrived, owned, rows, columns, 1, [own[:16, :HD]])
    far = swap_cores(give)
    near = unpack_rows(place, arrived, owned, rows, columns, 0, [give])
    grad_own, grad_other, across_low, across_high = attend(
        place, own, other, cotangent, near, far, own_weight, other_weight
    )
    lows, highs = scatter_ring(place, across_low, across_high, grad_own, grad_other, own_weight, other_weight)

    received = swap_cores(sum_columns(place, lows, highs))
    return sum_columns(place, lows, highs, received)


def solution(mesh):
    return jax.shard_map(
        shards,
        mesh=mesh,
        in_specs=(
            P("seq", "tp"),
            P("grp", None, "tp"),
            P("seq", None, "tp"),
            P("seq", None),
            P("seq", None),
            P("seq", "tp"),
        ),
        out_specs=P("seq", ("grp", "tp")),
        check_vma=False,
    )
```

```python
import jax
import jax.numpy as jnp
from jax import lax
from jax.experimental import pallas as pl
from jax.experimental.pallas import tpu as pltpu
from jax.sharding import PartitionSpec as P

HD = 128
GROUP = 64
KNB = 2
SCALE = HD ** (-0.5)
MIB = 1024 * 1024
BF16 = jnp.bfloat16


def dot_nt(a, b):
    return lax.dot_general(a, b, (((1,), (1,)), ((), ())), preferred_element_type=jnp.float32)


def dot_tn(a, b):
    return lax.dot_general(a, b, (((0,), (0,)), ((), ())), preferred_element_type=jnp.float32)


def dot_nn(a, b):
    return lax.dot_general(a, b, (((1,), (0,)), ((), ())), preferred_element_type=jnp.float32)


def params(mib=16):
    return pltpu.CompilerParams(vmem_limit_bytes=mib * MIB)


def cost(us):
    return pl.CostEstimate(flops=int(us * 1e9), bytes_accessed=int(us * 1e6), transcendentals=0)


def whole(shape):
    return pl.BlockSpec(shape, lambda *i: (0,) * len(shape))


def glance(array):
    return pl.BlockSpec((1,) * (array.ndim - 2) + (16, HD), lambda *i: (0,) * array.ndim)


def swap_cores(block):
    return lax.ppermute(block, "grp", [(0, 1), (1, 0)])


def swap(block, mask):
    count = lax.axis_size("tp")
    return lax.ppermute(block, "tp", [(i, i ^ mask) for i in range(count)])


TABLE = 8


def batch_of(owned):
    return 8 if owned % 8 == 0 else owned


def order_matrix(batch, parts, deep, back):
    size = batch * parts * deep
    row = lax.broadcasted_iota(jnp.int32, (size, size), 0)
    column = lax.broadcasted_iota(jnp.int32, (size, size), 1)
    travel, home = (column, row) if back else (row, column)
    where = (travel % batch) * (parts * deep) + travel // batch
    return (home == where).astype(jnp.float32).astype(BF16)


def table_rows(codes, owned):
    groups = codes.shape[1]
    group = lax.broadcasted_iota(jnp.int32, (groups, HD), 0)
    count = batch_of(owned) // (2 * KNB)
    core, group = group // (groups // 2), group % (groups // 2)
    number = KNB * (group // count * (2 * count) + core * count + group % count)
    column = lax.broadcasted_iota(jnp.int32, (groups, HD), 1)
    which = lax.broadcasted_iota(jnp.int32, (TABLE, HD), 0)
    table = jnp.zeros((TABLE, HD), jnp.float32)
    for i, values in enumerate((codes // 256, codes % 256)):
        values = values.astype(jnp.float32).astype(BF16)
        for k in range(KNB):
            spot = (column == number + k).astype(jnp.float32).astype(BF16)
            table = table + jnp.where(which == i, dot_nn(values, spot)[k : k + 1], 0.0)
    return table.astype(BF16)


def pack_kernel(batch, place_ref, codes_ref, neigh_ref, out_ref):
    owned, rows, half = neigh_ref.shape
    parts = out_ref.shape[0]
    deep = rows // parts
    chooser = order_matrix(batch, parts, deep, False)
    size = deep * batch
    for first in range(0, owned, batch):
        block = neigh_ref[first : first + batch].reshape(batch * rows, half)
        moved = dot_nn(chooser, block).astype(BF16).reshape(parts, size, half)
        for t in range(half // HD):
            start = (first // batch * (half // HD) + t) * size
            out_ref[:, start : start + size] = moved[:, :, t * HD : (t + 1) * HD]
    table = table_rows(codes_ref[...], owned)
    out_ref[:, owned * deep * half // HD :] = jnp.broadcast_to(table[None], (parts, TABLE, HD))


def pack_rows(place, codes, neighbours, parts):
    owned, rows, features = neighbours.shape
    half = features // 2
    message = owned * (rows // parts) * (half // HD) + TABLE
    batch = batch_of(owned)
    return pl.pallas_call(
        lambda *refs: pack_kernel(batch, *refs),
        grid_spec=pltpu.PrefetchScalarGridSpec(
            num_scalar_prefetch=1,
            grid=(1,),
            in_specs=[whole(codes.shape), pl.BlockSpec((owned, rows, half), lambda i, s: (0, 0, s[0]))],
            out_specs=whole((parts, message, HD)),
        ),
        out_shape=jax.ShapeDtypeStruct((parts, message, HD), BF16),
        compiler_params=params(16),
        cost_estimate=cost(3),
        name="pack_rows",
    )(place, codes, neighbours)


def route_kernel(owned, batch, columns, held_ref, *refs):
    out_ref = refs[-1]
    owners, message, _ = held_ref.shape
    size = (message - TABLE) * batch // (owned * columns)
    deep = size // batch
    total = owners * owned
    table = held_ref[:, message - TABLE :].astype(jnp.float32).reshape(owners * TABLE, HD).T
    held = []
    for first in range(0, owned, batch):
        pieces = []
        for t in range(columns):
            start = (first // batch * columns + t) * size
            block = held_ref[:, start : start + size].astype(jnp.float32)
            pieces += [block[:, r * batch : (r + 1) * batch].reshape(owners * batch, HD) for r in range(deep)]
        held.append(jnp.concatenate(pieces, axis=1).astype(BF16))
    held = jnp.concatenate(held, axis=0)
    lanes = lax.broadcasted_iota(jnp.int32, (owned, total), 1).astype(jnp.float32)
    per_dot = min(16, owners)
    for begin in range(0, owners, per_dot):
        choose = []
        for s in range(begin, begin + per_dot):
            high = table[:owned, s * TABLE : s * TABLE + 1]
            low = table[:owned, s * TABLE + 1 : s * TABLE + 2]
            choose.append((high * 256.0 + low == lanes).astype(jnp.float32))
        moved = dot_nn(jnp.concatenate(choose, axis=0).astype(BF16), held)
        moved = moved.reshape(per_dot, owned, columns * deep * HD)
        for first in range(0, owned, batch):
            for t in range(columns):
                start = (first // batch * columns + t) * size
                pieces = [
                    moved[:, first : first + batch, (t * deep + r) * HD : (t * deep + r + 1) * HD] for r in range(deep)
                ]
                out_ref[begin : begin + per_dot, start : start + size] = jnp.concatenate(pieces, axis=1).astype(BF16)


def route_rows(held, owned, columns, after):
    owners, message, _ = held.shape
    batch = batch_of(owned)
    out_shape = (owners, message - TABLE, HD)
    return pl.pallas_call(
        lambda *refs: route_kernel(owned, batch, columns, *refs),
        grid=(1,),
        out_shape=jax.ShapeDtypeStruct(out_shape, BF16),
        in_specs=[whole(held.shape)] + [glance(x) for x in after],
        out_specs=whole(out_shape),
        compiler_params=params(16),
        cost_estimate=cost(2),
        name="route_rows",
    )(held, *after)


def unpack_kernel(owned, batch, columns, partner, place_ref, arrived_ref, *refs):
    out_ref = refs[-1]
    parts, message, _ = arrived_ref.shape
    size = message * batch // (owned * columns)
    rows = parts * size // batch
    chooser = order_matrix(batch, parts, size // batch, True)
    count = batch // 2
    side = place_ref[0] ^ partner
    for first in range(0, owned, batch):
        starts = [(first // batch * columns + t) * size for t in range(columns)]
        block = jnp.concatenate([arrived_ref[:, x : x + size].reshape(parts * size, HD) for x in starts], axis=1)
        chosen = jnp.where(side == 0, chooser[: count * rows], chooser[count * rows :])
        out_ref[first // 2 * rows : (first // 2 + count) * rows] = dot_nn(chosen, block).astype(BF16)


def unpack_rows(place, arrived, owned, rows, columns, partner, after):
    batch = batch_of(owned)
    out_shape = (owned // 2 * rows, columns * HD)
    return pl.pallas_call(
        lambda *refs: unpack_kernel(owned, batch, columns, partner, *refs),
        grid_spec=pltpu.PrefetchScalarGridSpec(
            num_scalar_prefetch=1,
            grid=(1,),
            in_specs=[whole(arrived.shape)] + [glance(x) for x in after],
            out_specs=whole(out_shape),
        ),
        out_shape=jax.ShapeDtypeStruct(out_shape, BF16),
        compiler_params=params(16),
        cost_estimate=cost(1),
        name="unpack_rows",
    )(place, arrived, *after)


def project_kernel(place_ref, *refs):
    pieces, (own_w, other_w, own_out, other_out) = refs[:-4], refs[-4:]
    step = pl.program_id(0)
    for k in range(len(pieces) // 2):

        @pl.when(step == k)
        def _():
            block = jnp.concatenate([pieces[2 * k][...], pieces[2 * k + 1][...]])
            own = dot_nn(block, own_w[...])
            other = dot_nn(block, other_w[...])
            own_out[...] = own if k == 0 else own_out[...] + own
            other_out[...] = other if k == 0 else other_out[...] + other


def project_last_kernel(place_ref, *refs):
    pieces, (own_in, other_in, own_w, other_w, own_out, other_out) = refs[:-6], refs[-6:]
    block = jnp.concatenate([piece_ref[...] for piece_ref in pieces])
    own_out[...] = (own_in[...] + dot_nn(block, own_w[...])).astype(BF16)
    other_out[...] = (other_in[...] + dot_nn(block, other_w[...])).astype(BF16)


def project(place, masks, blocks, own_weight, other_weight, sums=None):
    depth = blocks[0].shape[1]
    width = own_weight.shape[1]
    final = sums is not None
    tokens = 2 * blocks[0].shape[0]

    def mask_of(k):
        return sum(jnp.where(k == i, m, 0) for i, m in enumerate(masks))

    weight_spec = pl.BlockSpec((depth, width), lambda k, s: (s[1] ^ mask_of(k), 0))
    out_spec = whole((tokens, width))
    shape = jax.ShapeDtypeStruct((tokens, width), BF16 if final else jnp.float32)
    return pl.pallas_call(
        project_last_kernel if final else project_kernel,
        grid_spec=pltpu.PrefetchScalarGridSpec(
            num_scalar_prefetch=1,
            grid=(len(masks),),
            in_specs=[whole(x.shape) for x in blocks] + [out_spec] * (2 * final) + [weight_spec] * 2,
            out_specs=[out_spec] * 2,
        ),
        out_shape=[shape, shape],
        compiler_params=params(24),
        cost_estimate=cost(2.5 * len(masks)),
        name="project",
    )(place, *blocks, *(sums or ()), own_weight, other_weight)


def heads_gradients(items):
    queries, memory, inputs, grad_out = zip(*items)
    count = range(len(items))
    scores = [dot_nt(memory[i], inputs[i]) * SCALE for i in count]
    scores = [jnp.exp(s - jnp.max(s, axis=0, keepdims=True)) for s in scores]
    enc_probs = [s * (1.0 / jnp.sum(s, axis=0, keepdims=True)) for s in scores]
    enc_weights = [p.astype(BF16) for p in enc_probs]
    mixed = [dot_tn(enc_weights[i], memory[i]) for i in count]
    keys = [(inputs[i].astype(jnp.float32) + mixed[i]).astype(BF16) for i in count]
    scores = [dot_nt(queries[i], keys[i]) * SCALE for i in count]
    grad_probs = [dot_nt(grad_out[i], keys[i]) for i in count]
    scores = [jnp.exp(s - jnp.max(s, axis=1, keepdims=True)) for s in scores]
    probs = [s * (1.0 / jnp.sum(s, axis=1, keepdims=True)) for s in scores]
    weights = [p.astype(BF16) for p in probs]
    from_values = [dot_tn(weights[i], grad_out[i]) for i in count]
    grad_scores = [p * (g - jnp.sum(p * g, axis=1, keepdims=True)) for p, g in zip(probs, grad_probs)]
    grad_scores = [g.astype(BF16) for g in grad_scores]
    grad_keys = [dot_tn(grad_scores[i], queries[i]) * SCALE + from_values[i] for i in count]
    grad_keys = [g.astype(BF16) for g in grad_keys]
    grad_queries = [(dot_nn(grad_scores[i], keys[i]) * SCALE).astype(BF16) for i in count]
    grad_probs = [dot_nt(memory[i], grad_keys[i]) for i in count]
    from_values = [dot_nn(enc_weights[i], grad_keys[i]) for i in count]
    grad_scores = [p * (g - jnp.sum(p * g, axis=0, keepdims=True)) for p, g in zip(enc_probs, grad_probs)]
    grad_scores = [g.astype(BF16) for g in grad_scores]
    grad_memory = [(dot_nn(grad_scores[i], inputs[i]) * SCALE + from_values[i]).astype(BF16) for i in count]
    return grad_queries, grad_memory


def attend_kernel(
    tp_count, place_ref, own_ref, other_ref, cot_ref, near_ref, far_ref, own_hbm, other_hbm,
    grad_own_ref, grad_other_ref, low_ref, high_ref, weights, arrived,
):
    step = pl.program_id(0)
    side = place_ref[0]
    columns = weights.shape[1]
    target = place_ref[1] ^ (tp_count // 2)
    copies = [
        pltpu.make_async_copy(
            hbm.at[pl.ds(pl.multiple_of((target + core * tp_count) * columns, columns), columns)],
            weights.at[2 * core + i],
            arrived.at[2 * core + i],
        )
        for core in range(2)
        for i, hbm in enumerate((own_hbm, other_hbm))
    ]

    @pl.when(step == 0)
    def _():
        for copy in copies:
            copy.start()

    half = near_ref.shape[1]
    first = side == 0
    tokens = own_ref.shape[0]
    groups = tokens // GROUP
    keys = near_ref.shape[0] // groups
    items, spots = [], []
    for c in range(groups):
        rows = slice(c * GROUP, (c + 1) * GROUP)
        place = pl.ds(pl.multiple_of(step * tokens + c * GROUP, GROUP), GROUP)
        for far, held_ref in enumerate((near_ref, far_ref)):
            start = ((side + far) % 2) * half
            for low in range(0, half, HD):
                lanes = pl.ds(pl.multiple_of(start + low, HD), HD)
                own = own_ref[rows, lanes]
                other = other_ref[rows, lanes]
                items.append(
                    (
                        jnp.where(first, own, other),
                        jnp.where(first, other, own),
                        held_ref[c * keys : (c + 1) * keys, low : low + HD],
                        cot_ref[rows, lanes],
                    )
                )
                spots.append((place, lanes))
    grad_queries, grad_memory = heads_gradients(items)
    for spot, grad_q, grad_m in zip(spots, grad_queries, grad_memory):
        grad_own_ref[spot] = jnp.where(first, grad_q, grad_m)
        grad_other_ref[spot] = jnp.where(first, grad_m, grad_q)

    @pl.when(step == pl.num_programs(0) - 1)
    def _():
        for copy in copies:
            copy.wait()
        low_rows = low_ref.shape[0]
        grad_own, grad_other = grad_own_ref[...], grad_other_ref[...]
        for core in range(2):
            term = dot_nt(grad_own, weights[2 * core]) + dot_nt(grad_other, weights[2 * core + 1])
            term = term.astype(BF16)
            low_ref[:, core * columns : (core + 1) * columns] = term[:low_rows]
            high_ref[:, core * columns : (core + 1) * columns] = term[low_rows:]


def attend(place, own, other, cotangent, near, far, own_weight, other_weight):
    tokens, width = own.shape
    rows, half = near.shape
    groups = tokens // GROUP
    steps = groups // 3 if groups % 3 == 0 else groups
    tp_count = lax.axis_size("tp")
    columns = own_weight.shape[0] // (2 * tp_count)
    token_spec = pl.BlockSpec((tokens // steps, width), lambda c, s: (c, 0))
    cot_spec = pl.BlockSpec((tokens // steps, width), lambda c, s: (s[0] * steps + c, 0))
    neigh_spec = pl.BlockSpec((rows // steps, half), lambda c, s: (c, 0))
    outs = [(tokens, width)] * 2 + [(tokens // 2, 2 * columns)] * 2
    return pl.pallas_call(
        lambda *refs: attend_kernel(tp_count, *refs),
        grid_spec=pltpu.PrefetchScalarGridSpec(
            num_scalar_prefetch=1,
            grid=(steps,),
            in_specs=[token_spec] * 2 + [cot_spec] + [neigh_spec] * 2 + [pl.BlockSpec(memory_space=pl.ANY)] * 2,
            out_specs=[whole(shape) for shape in outs],
            scratch_shapes=[pltpu.VMEM((4, columns, width), BF16), pltpu.SemaphoreType.DMA((4,))],
        ),
        out_shape=[jax.ShapeDtypeStruct(shape, BF16) for shape in outs],
        compiler_params=params(16),
        cost_estimate=cost(8),
        name="attend",
    )(place, own, other, cotangent, near, far, own_weight, other_weight)


def partial_kernel(masks, place_ref, own_ref, other_ref, own_a, own_b, other_a, other_b, *refs):
    out_refs = refs[-2 * len(masks) :]
    columns = own_a.shape[0]
    low_rows = own_ref.shape[0] // 2
    for i in range(len(masks)):

        @pl.when(pl.program_id(0) == i)
        def _():
            own, other = own_ref[...], other_ref[...]
            for core, weights in enumerate(((own_a, other_a), (own_b, other_b))):
                term = dot_nt(own, weights[0][...]) + dot_nt(other, weights[1][...])
                term = term.astype(BF16)
                place = slice(core * columns, (core + 1) * columns)
                out_refs[2 * i][:, place] = term[:low_rows]
                out_refs[2 * i + 1][:, place] = term[low_rows:]


def partial_terms(place, masks, grad_own, grad_other, own_weight, other_weight, after=()):
    tokens, width = grad_own.shape
    tp_count = lax.axis_size("tp")
    columns = own_weight.shape[0] // (2 * tp_count)

    def weight_spec(core):
        def index(i, s):
            mask = sum(jnp.where(i == u, mask, 0) for u, mask in enumerate(masks))
            return ((s[1] ^ mask) + core * tp_count, 0)

        return pl.BlockSpec((columns, width), index)

    shape = (tokens // 2, 2 * columns)
    return pl.pallas_call(
        lambda *refs: partial_kernel(masks, *refs),
        grid_spec=pltpu.PrefetchScalarGridSpec(
            num_scalar_prefetch=1,
            grid=(len(masks),),
            in_specs=[whole((tokens, width))] * 2
            + [weight_spec(0), weight_spec(1)] * 2
            + [glance(x) for x in after],
            out_specs=[whole(shape)] * (2 * len(masks)),
        ),
        out_shape=[jax.ShapeDtypeStruct(shape, BF16)] * (2 * len(masks)),
        compiler_params=params(16),
        cost_estimate=cost(2 * len(masks)),
        name="partial_terms",
    )(place, grad_own, grad_other, own_weight, own_weight, other_weight, other_weight, *after)


def add_kernel(*refs):
    count = len(refs) // 3
    for a_ref, b_ref, out_ref in zip(refs[:count], refs[count : 2 * count], refs[2 * count :]):
        out_ref[...] = (a_ref[...].astype(jnp.float32) + b_ref[...].astype(jnp.float32)).astype(BF16)


def add_terms(held, arrived):
    return pl.pallas_call(
        add_kernel,
        grid=(1,),
        out_shape=[jax.ShapeDtypeStruct(x.shape, BF16) for x in held],
        in_specs=[whole(x.shape) for x in (*held, *arrived)],
        out_specs=[whole(x.shape) for x in held],
        compiler_params=params(16),
        cost_estimate=cost(1),
        name="add_terms",
    )(*held, *arrived)


def scatter_ring(place, across_low, across_high, *operands):
    if lax.axis_size("tp") == 2:
        own_low, own_high = partial_terms(place, (0,), *operands)
        return [own_low, swap(across_low, 1)], [own_high, swap(across_high, 1)]
    from1 = swap(across_low, 1)
    from3 = swap(across_high, 3)
    low3, high3, low1, high1 = partial_terms(place, (3, 1), *operands)
    high3 = swap(high3, 3)
    low1 = swap(low1, 1)
    low3, high1 = add_terms((low3, high1), (from1, from3))
    own_low, own_high = partial_terms(place, (0,), *operands, after=(low3,))
    low3 = swap(low3, 3)
    high1 = swap(high1, 1)
    return [own_low, low1, low3], [own_high, high3, high1]


def sum_terms(terms):
    return sum(term[...].astype(jnp.float32) for term in terms).astype(BF16)


def columns_kernel(place_ref, *refs):
    terms, out_ref = refs[:-1], refs[-1]
    count, rows = len(terms) // 2, terms[0].shape[0]
    out_ref[:rows] = sum_terms(terms[:count])
    out_ref[rows:] = sum_terms(terms[count:])


def sum_columns(place, partner, lows, highs):
    rows, columns = lows[0].shape[0], lows[0].shape[1] // 2
    blocks = 1 if partner else 2
    return pl.pallas_call(
        columns_kernel,
        grid_spec=pltpu.PrefetchScalarGridSpec(
            num_scalar_prefetch=1,
            grid=(1,),
            in_specs=[pl.BlockSpec((rows, columns), lambda i, s: (0, s[0] ^ partner))] * len(lows + highs),
            out_specs=pl.BlockSpec((2 * rows, columns), lambda i, s: (0 if partner else s[0], 0)),
        ),
        out_shape=jax.ShapeDtypeStruct((2 * rows * blocks, columns), BF16),
        compiler_params=params(16),
        cost_estimate=cost(1),
        name="sum_columns",
    )(place, *lows, *highs)


def place_kernel(place_ref, received_ref, kept_ref, out_ref):
    out_ref[...] = received_ref[...]


def place_rows(place, received, kept):
    rows, columns = received.shape
    return pl.pallas_call(
        place_kernel,
        grid_spec=pltpu.PrefetchScalarGridSpec(
            num_scalar_prefetch=1,
            grid=(1,),
            in_specs=[whole(received.shape), pl.BlockSpec(memory_space=pl.ANY)],
            out_specs=pl.BlockSpec((rows, columns), lambda i, s: (1 - s[0], 0)),
        ),
        out_shape=jax.ShapeDtypeStruct(kept.shape, BF16),
        input_output_aliases={2: 0},
        compiler_params=params(16),
        cost_estimate=cost(1),
        name="place_rows",
    )(place, received, kept)


def shards(states, projections, neighbours, owner, slot, cotangent):
    side = lax.axis_index("grp").astype(jnp.int32)
    place = jnp.stack([side, lax.axis_index("tp").astype(jnp.int32)])
    shards_ = lax.axis_size("seq")
    tp_count = lax.axis_size("tp")
    tokens = states.shape[0] // 2
    owned, rows, features = neighbours.shape

    low = tokens // 2
    held = [lax.dynamic_slice_in_dim(states, side * tokens + first, low, 0) for first in (0, low)]
    if tp_count == 2:
        blocks, masks, early, last = held, [0], [], [swap(x, 1) for x in held]
    else:
        masks = [0, 1, 3]
        near1, near3 = ([swap(x, mask) for x in held] for mask in masks[1:])
        blocks = held + near1 + near3
        last = [swap(near3[0], 1), swap(near1[1], 3)]
        early = near1 + near3
    own_weight = projections[0]
    other_weight = swap_cores(own_weight)

    batch = batch_of(owned)
    columns = features // 2 // HD
    owner, slot = owner.T, slot.T
    codes = slot // batch * (shards_ * batch) + owner * batch + slot % batch
    packed = pack_rows(place, codes, neighbours, shards_)
    parts = lax.all_to_all(packed, "seq", split_axis=0, concat_axis=0, tiled=True)
    routed = route_rows(parts, owned, columns, [x[:16, :HD] for x in early])
    arrived = lax.all_to_all(routed, "seq", split_axis=0, concat_axis=0, tiled=True)

    sums = project(place, masks, blocks, own_weight, other_weight)
    own, other = project(place, [tp_count // 2], last, own_weight, other_weight, sums)
    give = unpack_rows(place, arrived, owned, rows, columns, 1, [own[:16, :HD]])
    far = swap_cores(give)
    near = unpack_rows(place, arrived, owned, rows, columns, 0, [give])
    grad_own, grad_other, across_low, across_high = attend(
        place, own, other, cotangent, near, far, own_weight, other_weight
    )
    lows, highs = scatter_ring(place, across_low, across_high, grad_own, grad_other, own_weight, other_weight)

    received = swap_cores(sum_columns(place, 1, lows, highs))
    return place_rows(place, received, sum_columns(place, 0, lows, highs))


def solution(mesh):
    return jax.shard_map(
        shards,
        mesh=mesh,
        in_specs=(
            P("seq", "tp"),
            P("grp", None, "tp"),
            P("seq", None, "tp"),
            P("seq", None),
            P("seq", None),
            P("seq", "tp"),
        ),
        out_specs=P("seq", ("grp", "tp")),
        check_vma=False,
    )
```

```python
import jax
import jax.numpy as jnp
from jax import lax
from jax.experimental import pallas as pl
from jax.experimental.pallas import tpu as pltpu
from jax.sharding import PartitionSpec as P

HD = 128
GROUP = 64
KNB = 2
SCALE = HD ** (-0.5)
MIB = 1024 * 1024
BF16 = jnp.bfloat16


def dot_nt(a, b):
    return lax.dot_general(a, b, (((1,), (1,)), ((), ())), preferred_element_type=jnp.float32)


def dot_tn(a, b):
    return lax.dot_general(a, b, (((0,), (0,)), ((), ())), preferred_element_type=jnp.float32)


def dot_nn(a, b):
    return lax.dot_general(a, b, (((1,), (0,)), ((), ())), preferred_element_type=jnp.float32)


def params(mib=16):
    return pltpu.CompilerParams(vmem_limit_bytes=mib * MIB)


def cost(us):
    return pl.CostEstimate(flops=int(us * 1e9), bytes_accessed=int(us * 1e6), transcendentals=0)


def whole(shape):
    return pl.BlockSpec(shape, lambda *i: (0,) * len(shape))


def glance(array):
    return pl.BlockSpec((1,) * (array.ndim - 2) + (16, HD), lambda *i: (0,) * array.ndim)


def swap_cores(block):
    return lax.ppermute(block, "grp", [(0, 1), (1, 0)])


def swap(block, mask):
    count = lax.axis_size("tp")
    return lax.ppermute(block, "tp", [(i, i ^ mask) for i in range(count)])


TABLE = 8


def batch_of(owned):
    return 8 if owned % 8 == 0 else owned


def order_matrix(batch, parts, deep, back):
    size = batch * parts * deep
    row = lax.broadcasted_iota(jnp.int32, (size, size), 0)
    column = lax.broadcasted_iota(jnp.int32, (size, size), 1)
    travel, home = (column, row) if back else (row, column)
    where = (travel % batch) * (parts * deep) + travel // batch
    return (home == where).astype(jnp.float32).astype(BF16)


def table_rows(codes, owned):
    groups = codes.shape[1]
    group = lax.broadcasted_iota(jnp.int32, (groups, HD), 0)
    count = batch_of(owned) // (2 * KNB)
    core, group = group // (groups // 2), group % (groups // 2)
    number = KNB * (group // count * (2 * count) + core * count + group % count)
    column = lax.broadcasted_iota(jnp.int32, (groups, HD), 1)
    which = lax.broadcasted_iota(jnp.int32, (TABLE, HD), 0)
    table = jnp.zeros((TABLE, HD), jnp.float32)
    for i, values in enumerate((codes // 256, codes % 256)):
        values = values.astype(jnp.float32).astype(BF16)
        for k in range(KNB):
            spot = (column == number + k).astype(jnp.float32).astype(BF16)
            table = table + jnp.where(which == i, dot_nn(values, spot)[k : k + 1], 0.0)
    return table.astype(BF16)


def pack_kernel(batch, place_ref, codes_ref, neigh_ref, out_ref):
    owned, rows, half = neigh_ref.shape
    parts = out_ref.shape[0]
    deep = rows // parts
    chooser = order_matrix(batch, parts, deep, False)
    size = deep * batch
    for first in range(0, owned, batch):
        block = neigh_ref[first : first + batch].reshape(batch * rows, half)
        moved = dot_nn(chooser, block).astype(BF16).reshape(parts, size, half)
        for t in range(half // HD):
            start = (first // batch * (half // HD) + t) * size
            out_ref[:, start : start + size] = moved[:, :, t * HD : (t + 1) * HD]
    table = table_rows(codes_ref[...], owned)
    out_ref[:, owned * deep * half // HD :] = jnp.broadcast_to(table[None], (parts, TABLE, HD))


def pack_rows(place, codes, neighbours, parts):
    owned, rows, features = neighbours.shape
    half = features // 2
    message = owned * (rows // parts) * (half // HD) + TABLE
    batch = batch_of(owned)
    return pl.pallas_call(
        lambda *refs: pack_kernel(batch, *refs),
        grid_spec=pltpu.PrefetchScalarGridSpec(
            num_scalar_prefetch=1,
            grid=(1,),
            in_specs=[whole(codes.shape), pl.BlockSpec((owned, rows, half), lambda i, s: (0, 0, s[0]))],
            out_specs=whole((parts, message, HD)),
        ),
        out_shape=jax.ShapeDtypeStruct((parts, message, HD), BF16),
        compiler_params=params(16),
        cost_estimate=cost(3),
        name="pack_rows",
    )(place, codes, neighbours)


def route_kernel(owned, batch, columns, held_ref, *refs):
    out_ref = refs[-1]
    owners, message, _ = held_ref.shape
    size = (message - TABLE) * batch // (owned * columns)
    deep = size // batch
    total = owners * owned
    table = held_ref[:, message - TABLE :].astype(jnp.float32).reshape(owners * TABLE, HD).T
    held = []
    for first in range(0, owned, batch):
        pieces = []
        for t in range(columns):
            start = (first // batch * columns + t) * size
            block = held_ref[:, start : start + size].astype(jnp.float32)
            pieces += [block[:, r * batch : (r + 1) * batch].reshape(owners * batch, HD) for r in range(deep)]
        held.append(jnp.concatenate(pieces, axis=1).astype(BF16))
    held = jnp.concatenate(held, axis=0)
    lanes = lax.broadcasted_iota(jnp.int32, (owned, total), 1).astype(jnp.float32)
    per_dot = min(32, owners)
    for begin in range(0, owners, per_dot):
        choose = []
        for s in range(begin, begin + per_dot):
            high = table[:owned, s * TABLE : s * TABLE + 1]
            low = table[:owned, s * TABLE + 1 : s * TABLE + 2]
            choose.append((high * 256.0 + low == lanes).astype(jnp.float32))
        moved = dot_nn(jnp.concatenate(choose, axis=0).astype(BF16), held)
        moved = moved.reshape(per_dot, owned, columns * deep * HD)
        for first in range(0, owned, batch):
            for t in range(columns):
                start = (first // batch * columns + t) * size
                pieces = [
                    moved[:, first : first + batch, (t * deep + r) * HD : (t * deep + r + 1) * HD] for r in range(deep)
                ]
                out_ref[begin : begin + per_dot, start : start + size] = jnp.concatenate(pieces, axis=1).astype(BF16)


def route_rows(held, owned, columns, after):
    owners, message, _ = held.shape
    batch = batch_of(owned)
    out_shape = (owners, message - TABLE, HD)
    return pl.pallas_call(
        lambda *refs: route_kernel(owned, batch, columns, *refs),
        grid=(1,),
        out_shape=jax.ShapeDtypeStruct(out_shape, BF16),
        in_specs=[whole(held.shape)] + [glance(x) for x in after],
        out_specs=whole(out_shape),
        compiler_params=params(16),
        cost_estimate=cost(2),
        name="route_rows",
    )(held, *after)


def unpack_kernel(owned, batch, columns, partner, place_ref, arrived_ref, *refs):
    out_ref = refs[-1]
    parts, message, _ = arrived_ref.shape
    size = message * batch // (owned * columns)
    rows = parts * size // batch
    chooser = order_matrix(batch, parts, size // batch, True)
    count = batch // 2
    side = place_ref[0] ^ partner
    for first in range(0, owned, batch):
        starts = [(first // batch * columns + t) * size for t in range(columns)]
        block = jnp.concatenate([arrived_ref[:, x : x + size].reshape(parts * size, HD) for x in starts], axis=1)
        chosen = jnp.where(side == 0, chooser[: count * rows], chooser[count * rows :])
        out_ref[first // 2 * rows : (first // 2 + count) * rows] = dot_nn(chosen, block).astype(BF16)


def unpack_rows(place, arrived, owned, rows, columns, partner, after):
    batch = batch_of(owned)
    out_shape = (owned // 2 * rows, columns * HD)
    return pl.pallas_call(
        lambda *refs: unpack_kernel(owned, batch, columns, partner, *refs),
        grid_spec=pltpu.PrefetchScalarGridSpec(
            num_scalar_prefetch=1,
            grid=(1,),
            in_specs=[whole(arrived.shape)] + [glance(x) for x in after],
            out_specs=whole(out_shape),
        ),
        out_shape=jax.ShapeDtypeStruct(out_shape, BF16),
        compiler_params=params(16),
        cost_estimate=cost(1),
        name="unpack_rows",
    )(place, arrived, *after)


def project_kernel(place_ref, *refs):
    pieces, (own_w, other_w, own_out, other_out) = refs[:-4], refs[-4:]
    step = pl.program_id(0)
    for k in range(len(pieces) // 2):

        @pl.when(step == k)
        def _():
            block = jnp.concatenate([pieces[2 * k][...], pieces[2 * k + 1][...]])
            own = dot_nn(block, own_w[...])
            other = dot_nn(block, other_w[...])
            own_out[...] = own if k == 0 else own_out[...] + own
            other_out[...] = other if k == 0 else other_out[...] + other


def project_last_kernel(place_ref, *refs):
    pieces, (own_in, other_in, own_w, other_w, own_out, other_out) = refs[:-6], refs[-6:]
    block = jnp.concatenate([piece_ref[...] for piece_ref in pieces])
    own_out[...] = (own_in[...] + dot_nn(block, own_w[...])).astype(BF16)
    other_out[...] = (other_in[...] + dot_nn(block, other_w[...])).astype(BF16)


def project(place, masks, blocks, own_weight, other_weight, sums=None):
    depth = blocks[0].shape[1]
    width = own_weight.shape[1]
    final = sums is not None
    tokens = 2 * blocks[0].shape[0]

    def mask_of(k):
        return sum(jnp.where(k == i, m, 0) for i, m in enumerate(masks))

    weight_spec = pl.BlockSpec((depth, width), lambda k, s: (s[1] ^ mask_of(k), 0))
    out_spec = whole((tokens, width))
    shape = jax.ShapeDtypeStruct((tokens, width), BF16 if final else jnp.float32)
    return pl.pallas_call(
        project_last_kernel if final else project_kernel,
        grid_spec=pltpu.PrefetchScalarGridSpec(
            num_scalar_prefetch=1,
            grid=(len(masks),),
            in_specs=[whole(x.shape) for x in blocks] + [out_spec] * (2 * final) + [weight_spec] * 2,
            out_specs=[out_spec] * 2,
        ),
        out_shape=[shape, shape],
        compiler_params=params(24),
        cost_estimate=cost(2.5 * len(masks)),
        name="project",
    )(place, *blocks, *(sums or ()), own_weight, other_weight)


def heads_gradients(items):
    queries, memory, inputs, grad_out = zip(*items)
    count = range(len(items))
    scores = [dot_nt(memory[i], inputs[i]) * SCALE for i in count]
    scores = [jnp.exp(s - jnp.max(s, axis=0, keepdims=True)) for s in scores]
    enc_probs = [s * (1.0 / jnp.sum(s, axis=0, keepdims=True)) for s in scores]
    enc_weights = [p.astype(BF16) for p in enc_probs]
    mixed = [dot_tn(enc_weights[i], memory[i]) for i in count]
    keys = [(inputs[i].astype(jnp.float32) + mixed[i]).astype(BF16) for i in count]
    scores = [dot_nt(queries[i], keys[i]) * SCALE for i in count]
    grad_probs = [dot_nt(grad_out[i], keys[i]) for i in count]
    scores = [jnp.exp(s - jnp.max(s, axis=1, keepdims=True)) for s in scores]
    probs = [s * (1.0 / jnp.sum(s, axis=1, keepdims=True)) for s in scores]
    weights = [p.astype(BF16) for p in probs]
    from_values = [dot_tn(weights[i], grad_out[i]) for i in count]
    grad_scores = [p * (g - jnp.sum(p * g, axis=1, keepdims=True)) for p, g in zip(probs, grad_probs)]
    grad_scores = [g.astype(BF16) for g in grad_scores]
    grad_keys = [dot_tn(grad_scores[i], queries[i]) * SCALE + from_values[i] for i in count]
    grad_keys = [g.astype(BF16) for g in grad_keys]
    grad_queries = [(dot_nn(grad_scores[i], keys[i]) * SCALE).astype(BF16) for i in count]
    grad_probs = [dot_nt(memory[i], grad_keys[i]) for i in count]
    from_values = [dot_nn(enc_weights[i], grad_keys[i]) for i in count]
    grad_scores = [p * (g - jnp.sum(p * g, axis=0, keepdims=True)) for p, g in zip(enc_probs, grad_probs)]
    grad_scores = [g.astype(BF16) for g in grad_scores]
    grad_memory = [(dot_nn(grad_scores[i], inputs[i]) * SCALE + from_values[i]).astype(BF16) for i in count]
    return grad_queries, grad_memory


def attend_kernel(
    tp_count, place_ref, own_ref, other_ref, cot_ref, near_ref, far_ref, own_hbm, other_hbm,
    grad_own_ref, grad_other_ref, low_ref, high_ref, weights, arrived,
):
    step = pl.program_id(0)
    side = place_ref[0]
    columns = weights.shape[1]
    target = place_ref[1] ^ (tp_count // 2)
    copies = [
        pltpu.make_async_copy(
            hbm.at[pl.ds(pl.multiple_of((target + core * tp_count) * columns, columns), columns)],
            weights.at[2 * core + i],
            arrived.at[2 * core + i],
        )
        for core in range(2)
        for i, hbm in enumerate((own_hbm, other_hbm))
    ]

    @pl.when(step == 0)
    def _():
        for copy in copies:
            copy.start()

    half = near_ref.shape[1]
    first = side == 0
    tokens = own_ref.shape[0]
    groups = tokens // GROUP
    keys = near_ref.shape[0] // groups
    items, spots = [], []
    for c in range(groups):
        rows = slice(c * GROUP, (c + 1) * GROUP)
        place = pl.ds(pl.multiple_of(step * tokens + c * GROUP, GROUP), GROUP)
        for far, held_ref in enumerate((near_ref, far_ref)):
            start = ((side + far) % 2) * half
            for low in range(0, half, HD):
                lanes = pl.ds(pl.multiple_of(start + low, HD), HD)
                own = own_ref[rows, lanes]
                other = other_ref[rows, lanes]
                items.append(
                    (
                        jnp.where(first, own, other),
                        jnp.where(first, other, own),
                        held_ref[c * keys : (c + 1) * keys, low : low + HD],
                        cot_ref[rows, lanes],
                    )
                )
                spots.append((place, lanes))
    grad_queries, grad_memory = heads_gradients(items)
    for spot, grad_q, grad_m in zip(spots, grad_queries, grad_memory):
        grad_own_ref[spot] = jnp.where(first, grad_q, grad_m)
        grad_other_ref[spot] = jnp.where(first, grad_m, grad_q)

    @pl.when(step == pl.num_programs(0) - 1)
    def _():
        for copy in copies:
            copy.wait()
        low_rows = low_ref.shape[0]
        grad_own, grad_other = grad_own_ref[...], grad_other_ref[...]
        for core in range(2):
            term = dot_nt(grad_own, weights[2 * core]) + dot_nt(grad_other, weights[2 * core + 1])
            term = term.astype(BF16)
            low_ref[:, core * columns : (core + 1) * columns] = term[:low_rows]
            high_ref[:, core * columns : (core + 1) * columns] = term[low_rows:]


def attend(place, own, other, cotangent, near, far, own_weight, other_weight):
    tokens, width = own.shape
    rows, half = near.shape
    groups = tokens // GROUP
    steps = groups // 3 if groups % 3 == 0 else groups
    tp_count = lax.axis_size("tp")
    columns = own_weight.shape[0] // (2 * tp_count)
    token_spec = pl.BlockSpec((tokens // steps, width), lambda c, s: (c, 0))
    cot_spec = pl.BlockSpec((tokens // steps, width), lambda c, s: (s[0] * steps + c, 0))
    neigh_spec = pl.BlockSpec((rows // steps, half), lambda c, s: (c, 0))
    outs = [(tokens, width)] * 2 + [(tokens // 2, 2 * columns)] * 2
    return pl.pallas_call(
        lambda *refs: attend_kernel(tp_count, *refs),
        grid_spec=pltpu.PrefetchScalarGridSpec(
            num_scalar_prefetch=1,
            grid=(steps,),
            in_specs=[token_spec] * 2 + [cot_spec] + [neigh_spec] * 2 + [pl.BlockSpec(memory_space=pl.ANY)] * 2,
            out_specs=[whole(shape) for shape in outs],
            scratch_shapes=[pltpu.VMEM((4, columns, width), BF16), pltpu.SemaphoreType.DMA((4,))],
        ),
        out_shape=[jax.ShapeDtypeStruct(shape, BF16) for shape in outs],
        compiler_params=params(16),
        cost_estimate=cost(8),
        name="attend",
    )(place, own, other, cotangent, near, far, own_weight, other_weight)


def partial_kernel(masks, place_ref, own_ref, other_ref, own_a, own_b, other_a, other_b, *refs):
    out_refs = refs[-2 * len(masks) :]
    columns = own_a.shape[0]
    low_rows = own_ref.shape[0] // 2
    for i in range(len(masks)):

        @pl.when(pl.program_id(0) == i)
        def _():
            own, other = own_ref[...], other_ref[...]
            for core, weights in enumerate(((own_a, other_a), (own_b, other_b))):
                term = dot_nt(own, weights[0][...]) + dot_nt(other, weights[1][...])
                term = term.astype(BF16)
                place = slice(core * columns, (core + 1) * columns)
                out_refs[2 * i][:, place] = term[:low_rows]
                out_refs[2 * i + 1][:, place] = term[low_rows:]


def partial_terms(place, masks, grad_own, grad_other, own_weight, other_weight, after=()):
    tokens, width = grad_own.shape
    tp_count = lax.axis_size("tp")
    columns = own_weight.shape[0] // (2 * tp_count)

    def weight_spec(core):
        def index(i, s):
            mask = sum(jnp.where(i == u, mask, 0) for u, mask in enumerate(masks))
            return ((s[1] ^ mask) + core * tp_count, 0)

        return pl.BlockSpec((columns, width), index)

    shape = (tokens // 2, 2 * columns)
    return pl.pallas_call(
        lambda *refs: partial_kernel(masks, *refs),
        grid_spec=pltpu.PrefetchScalarGridSpec(
            num_scalar_prefetch=1,
            grid=(len(masks),),
            in_specs=[whole((tokens, width))] * 2
            + [weight_spec(0), weight_spec(1)] * 2
            + [glance(x) for x in after],
            out_specs=[whole(shape)] * (2 * len(masks)),
        ),
        out_shape=[jax.ShapeDtypeStruct(shape, BF16)] * (2 * len(masks)),
        compiler_params=params(16),
        cost_estimate=cost(2 * len(masks)),
        name="partial_terms",
    )(place, grad_own, grad_other, own_weight, own_weight, other_weight, other_weight, *after)


def add_kernel(*refs):
    count = len(refs) // 3
    for a_ref, b_ref, out_ref in zip(refs[:count], refs[count : 2 * count], refs[2 * count :]):
        out_ref[...] = (a_ref[...].astype(jnp.float32) + b_ref[...].astype(jnp.float32)).astype(BF16)


def add_terms(held, arrived):
    return pl.pallas_call(
        add_kernel,
        grid=(1,),
        out_shape=[jax.ShapeDtypeStruct(x.shape, BF16) for x in held],
        in_specs=[whole(x.shape) for x in (*held, *arrived)],
        out_specs=[whole(x.shape) for x in held],
        compiler_params=params(16),
        cost_estimate=cost(1),
        name="add_terms",
    )(*held, *arrived)


def scatter_ring(place, across_low, across_high, *operands):
    if lax.axis_size("tp") == 2:
        own_low, own_high = partial_terms(place, (0,), *operands)
        return [own_low, swap(across_low, 1)], [own_high, swap(across_high, 1)]
    from1 = swap(across_low, 1)
    from3 = swap(across_high, 3)
    low3, high3, low1, high1 = partial_terms(place, (3, 1), *operands)
    high3 = swap(high3, 3)
    low1 = swap(low1, 1)
    low3, high1 = add_terms((low3, high1), (from1, from3))
    own_low, own_high = partial_terms(place, (0,), *operands, after=(low3,))
    low3 = swap(low3, 3)
    high1 = swap(high1, 1)
    return [own_low, low1, low3], [own_high, high3, high1]


def sum_terms(terms):
    return sum(term[...].astype(jnp.float32) for term in terms).astype(BF16)


def columns_kernel(place_ref, *refs):
    terms, out_ref = refs[:-1], refs[-1]
    count, rows = len(terms) // 2, terms[0].shape[0]
    out_ref[:rows] = sum_terms(terms[:count])
    out_ref[rows:] = sum_terms(terms[count:])


def sum_columns(place, partner, lows, highs):
    rows, columns = lows[0].shape[0], lows[0].shape[1] // 2
    blocks = 1 if partner else 2
    return pl.pallas_call(
        columns_kernel,
        grid_spec=pltpu.PrefetchScalarGridSpec(
            num_scalar_prefetch=1,
            grid=(1,),
            in_specs=[pl.BlockSpec((rows, columns), lambda i, s: (0, s[0] ^ partner))] * len(lows + highs),
            out_specs=pl.BlockSpec((2 * rows, columns), lambda i, s: (0 if partner else s[0], 0)),
        ),
        out_shape=jax.ShapeDtypeStruct((2 * rows * blocks, columns), BF16),
        compiler_params=params(16),
        cost_estimate=cost(1),
        name="sum_columns",
    )(place, *lows, *highs)


def place_kernel(place_ref, received_ref, kept_ref, out_ref):
    out_ref[...] = received_ref[...]


def place_rows(place, received, kept):
    rows, columns = received.shape
    return pl.pallas_call(
        place_kernel,
        grid_spec=pltpu.PrefetchScalarGridSpec(
            num_scalar_prefetch=1,
            grid=(1,),
            in_specs=[whole(received.shape), pl.BlockSpec(memory_space=pl.ANY)],
            out_specs=pl.BlockSpec((rows, columns), lambda i, s: (1 - s[0], 0)),
        ),
        out_shape=jax.ShapeDtypeStruct(kept.shape, BF16),
        input_output_aliases={2: 0},
        compiler_params=params(16),
        cost_estimate=cost(1),
        name="place_rows",
    )(place, received, kept)


def shards(states, projections, neighbours, owner, slot, cotangent):
    side = lax.axis_index("grp").astype(jnp.int32)
    place = jnp.stack([side, lax.axis_index("tp").astype(jnp.int32)])
    shards_ = lax.axis_size("seq")
    tp_count = lax.axis_size("tp")
    tokens = states.shape[0] // 2
    owned, rows, features = neighbours.shape

    low = tokens // 2
    held = [lax.dynamic_slice_in_dim(states, side * tokens + first, low, 0) for first in (0, low)]
    if tp_count == 2:
        blocks, masks, early, last = held, [0], [], [swap(x, 1) for x in held]
    else:
        masks = [0, 1, 3]
        near1, near3 = ([swap(x, mask) for x in held] for mask in masks[1:])
        blocks = held + near1 + near3
        last = [swap(near3[0], 1), swap(near1[1], 3)]
        early = near1 + near3
    own_weight = projections[0]
    other_weight = swap_cores(own_weight)

    batch = batch_of(owned)
    columns = features // 2 // HD
    owner, slot = owner.T, slot.T
    codes = slot // batch * (shards_ * batch) + owner * batch + slot % batch
    packed = pack_rows(place, codes, neighbours, shards_)
    parts = lax.all_to_all(packed, "seq", split_axis=0, concat_axis=0, tiled=True)
    routed = route_rows(parts, owned, columns, [x[:16, :HD] for x in early])
    arrived = lax.all_to_all(routed, "seq", split_axis=0, concat_axis=0, tiled=True)

    sums = project(place, masks, blocks, own_weight, other_weight)
    own, other = project(place, [tp_count // 2], last, own_weight, other_weight, sums)
    give = unpack_rows(place, arrived, owned, rows, columns, 1, [own[:16, :HD]])
    far = swap_cores(give)
    near = unpack_rows(place, arrived, owned, rows, columns, 0, [give])
    grad_own, grad_other, across_low, across_high = attend(
        place, own, other, cotangent, near, far, own_weight, other_weight
    )
    lows, highs = scatter_ring(place, across_low, across_high, grad_own, grad_other, own_weight, other_weight)

    received = swap_cores(sum_columns(place, 1, lows, highs))
    return place_rows(place, received, sum_columns(place, 0, lows, highs))


def solution(mesh):
    return jax.shard_map(
        shards,
        mesh=mesh,
        in_specs=(
            P("seq", "tp"),
            P("grp", None, "tp"),
            P("seq", None, "tp"),
            P("seq", None),
            P("seq", None),
            P("seq", "tp"),
        ),
        out_specs=P("seq", ("grp", "tp")),
        check_vma=False,
    )
```
